512 devices in a mesh: team: 4 (over y_hi), blk: 128 (over x, y_lo, z, core).
Axes of the slice: x: 4, y: 8 (y_hi: 4, y_lo: 2; y = y_hi * 2 + y_lo), z: 8, core: 2. Of those that a mesh axis runs over, the one named last changes fastest.
Arguments:
- position: float32 [3, 131072], P(None, ('team', 'blk')), may hold values from -6 to 6
- velocity: float32 [3, 131072], P(None, ('team', 'blk')), may hold values from -6 to 6
- old_accel: float32 [3, 131072], P(None, ('team', 'blk')), may hold values from -6 to 6
- old_jerk: float32 [3, 131072], P(None, ('team', 'blk')), may hold values from -6 to 6
- mass: float32 [131072], P(('team', 'blk')), may hold values from 1.5258789e-06 to 3.8146973e-05
- elapsed: float32 [131072], P(('team', 'blk')), may hold values from 0.0625 to 0.5
- active_slot: int32 [16384], P('blk'), may hold values from 0 to 255, as said below
- active_owner: int32 [16384], P('blk'), may hold values from 0 to 3
Outputs:
- phase: float32 [6, 16384], P(None, 'blk')
- force: float32 [6, 16384], P(None, 'blk')
- higher: float32 [6, 16384], P(None, 'blk')
The draws below stay inside these ranges and needn't reach their ends.
Inputs may be any that keep to these rules, and one draw needn't show every extreme that they name: Within each block of 128 active entries the pairs (active_owner, active_slot) are all different; slot 255 of owner 3 and slot 0 of owner 0 are active in every block.
All inputs are finite; a program needn't handle non-finite values.
Results may differ from the reference program's by a relative error of at most 0.0003.
Values sent between devices are 32-bit elements; how exact they have to be, the bound alone decides.
No kernel may reach another device: no remote copies, remote signals or barrier semaphores. Data moves between devices by JAX's collectives and lax.ppermute only.
A program may use at most 64 MiB of HBM per device.

```python
import math
import jax
import jax.numpy as jnp
from jax import lax

J_DEV = 256
A_DEV = 128
NSTARS = 131072
N_ACT = 16384
N_TEAM = 4
N_BLK = 128


def picked_stars(key):
    nblock = N_ACT // A_DEV
    column = N_TEAM * J_DEV

    def one_block(sub):
        first, second = jax.random.split(sub)
        others = jax.random.permutation(first, column - 2)[:A_DEV - 2] + 1
        full = jnp.concatenate([jnp.array([column - 1, 0], dtype=jnp.int32), others.astype(jnp.int32)])
        return full[jax.random.permutation(second, A_DEV)]
    keys = jax.random.split(key, nblock)
    return jax.vmap(one_block)(keys).reshape(-1).astype(jnp.int32)


def draw_active_slot(key, part):
    chosen = picked_stars(key)
    return (chosen % J_DEV).astype(jnp.int32)


def draw_active_owner(key, part):
    chosen = picked_stars(key)
    return (chosen // J_DEV).astype(jnp.int32)


def block_scale(own_key, dims, pieces, smallest, high):
    level = 1.0
    for dim, shards_of in pieces:
        heights = jax.random.uniform(jax.random.fold_in(jax.random.fold_in(own_key, 6), dim), (shards_of,), jnp.float32, smallest / len(pieces), high / len(pieces))
        level = level * jnp.repeat(jnp.exp(heights), dims[dim] // shards_of).reshape((-1,) + (1,) * (len(dims) - 1 - dim))
    return level


def noise(rng, extent, deviation, limit, pieces=(), kind=jnp.bfloat16):
    result = deviation * jax.random.normal(rng, extent, jnp.float32)
    if pieces:
        result = result * block_scale(rng, extent, pieces, -0.22, 0.18)
    return jnp.clip(result, -limit, limit).astype(kind)


def setup_inputs(seed: int = 0) -> dict:
    key_of = jax.random.split(jax.random.key(seed), 9)
    position = noise(key_of[0], (3, NSTARS), 1.0, 6.0, ((1, 512),), jnp.float32)
    velocity = noise(key_of[1], (3, NSTARS), 0.5, 6.0, ((1, 512),), jnp.float32)
    old_accel = noise(key_of[2], (3, NSTARS), 1.0, 6.0, ((1, 512),), jnp.float32)
    old_jerk = noise(key_of[3], (3, NSTARS), 1.0, 6.0, ((1, 512),), jnp.float32)
    mass = jnp.clip(jnp.exp(math.log(3.814697265625e-05) - 3.218876 * jax.random.uniform(key_of[4], (NSTARS,), jnp.float32) ** block_scale(key_of[4], (NSTARS,), ((0, 512),), -0.2, 0.2)), 1.5258789289873675e-06, 3.814697265625e-05)
    elapsed = jnp.clip(jnp.exp(math.log(0.5) - 2.0794415 * jax.random.uniform(key_of[5], (NSTARS,), jnp.float32) ** block_scale(key_of[5], (NSTARS,), ((0, 512),), -0.2, 0.2)), 0.0625, 0.5)
    active_slot = draw_active_slot(jax.random.fold_in(key_of[8], 71), 0)
    active_owner = draw_active_owner(jax.random.fold_in(key_of[8], 71), 0)
    return dict(position=position, velocity=velocity, old_accel=old_accel, old_jerk=old_jerk, mass=mass, elapsed=elapsed, active_slot=active_slot, active_owner=active_owner)


SOFTEN2 = 0.0001

def predict(x, v, a, j, h):
    xp = x + h * (v + h * (a / 2.0 + h * j / 6.0))
    vp = v + h * (a + h * j / 2.0)
    return (xp, vp)

def pair_block(ipack, jpack):
    dx = jpack[0:3, None, :] - ipack[0:3, :, None]
    dv = jpack[3:6, None, :] - ipack[3:6, :, None]
    r2 = lax.optimization_barrier(jnp.sum(dx * dx, axis=0)) + SOFTEN2
    inv = 1.0 / jnp.sqrt(r2)
    weight = jpack[6][None, :] * inv * inv * inv
    rv = 3.0 * lax.optimization_barrier(jnp.sum(dx * dv, axis=0)) / r2
    acc = lax.optimization_barrier(jnp.sum(weight * dx, axis=2))
    jerk = lax.optimization_barrier(jnp.sum(weight * (dv - rv * dx), axis=2))
    return jnp.concatenate([acc, jerk], axis=0)

def correct(own, total):
    x0, v0, a0, j0, dt = (own[0:3], own[3:6], own[6:9], own[9:12], own[12:13])
    a1, j1 = (total[0:3], total[3:6])
    v1 = v0 + (a0 + a1) * dt / 2.0 + (j0 - j1) * dt * dt / 12.0
    x1 = x0 + (v0 + v1) * dt / 2.0 + (a0 - a1) * dt * dt / 12.0
    snap = -6.0 * (a0 - a1) - dt * (4.0 * j0 + 2.0 * j1)
    crackle = 12.0 * (a0 - a1) + 6.0 * dt * (j0 + j1)
    return (jnp.concatenate([x1, v1], 0), total, jnp.concatenate([snap, crackle], 0))

def reference(position, velocity, old_accel, old_jerk, mass, elapsed, active_slot, active_owner):
    block = jnp.arange(N_ACT, dtype=jnp.int32) // A_DEV
    star = (active_owner * N_BLK + block) * J_DEV + active_slot
    state = jnp.concatenate([position, velocity, old_accel, old_jerk, elapsed[None, :]], axis=0)
    own = jnp.take(state, star.astype(jnp.int32), axis=1)
    xp, vp = predict(position, velocity, old_accel, old_jerk, elapsed[None, :])
    jpack = jnp.concatenate([xp, vp, mass[None, :]], axis=0)
    xi, vi = predict(own[0:3], own[3:6], own[6:9], own[9:12], own[12:13])
    ipack = jnp.concatenate([xi, vi], axis=0)
    blocks = ipack.reshape(6, N_BLK, A_DEV).transpose(1, 0, 2)
    total = lax.map(lambda one: pair_block(one, jpack), blocks)
    total = total.transpose(1, 0, 2).reshape(6, N_ACT)
    return correct(own, total)
```

```python
import functools
import jax
import jax.numpy as jnp
from jax import lax
from jax.experimental import pallas as pl
from jax.experimental.pallas import tpu as pltpu
from jax.sharding import Mesh, PartitionSpec as P

SOFTEN2 = 0.0001
N_X, N_YLO, N_Z, N_CORE = 4, 2, 8, 2
LANES = 128
GATHER = ("x", "z")
REDUCE = ("team", "y", "core")


def predict(x, v, a, j, h):
    xp = x + h * (v + h * (a / 2.0 + h * j / 6.0))
    vp = v + h * (a + h * j / 2.0)
    return (xp, vp)


def pack_kernel(x_ref, v_ref, a_ref, j_ref, m_ref, h_ref, slot_ref, owner_ref, stars_ref, state_ref):
    x, v, a, j, m, h = (x_ref[...], v_ref[...], a_ref[...], j_ref[...], m_ref[...], h_ref[...])
    xp, vp = predict(x, v, a, j, h)
    members = x.shape[1]
    actives = slot_ref.shape[1]
    star = jnp.concatenate([xp, vp, m, jnp.zeros((1, members), jnp.float32)], axis=0)
    for k in range(stars_ref.shape[0]):
        stars_ref[k] = star
    team = lax.axis_index("team")
    wanted = jnp.where(owner_ref[...] == team, slot_ref[...], -1)
    chooser = (lax.broadcasted_iota(jnp.int32, (members, actives), 0) == wanted).astype(jnp.float32)
    state = jnp.concatenate([x, v, a, j, h, jnp.zeros((3, members), jnp.float32)], axis=0)
    chosen = jnp.dot(state, chooser, precision=lax.Precision.HIGHEST, preferred_element_type=jnp.float32)
    for k in range(state_ref.shape[0]):
        state_ref[k] = chosen


def force_kernel(stars_ref, state_ref, out_ref, row_ref, col_ref, acc_ref):
    n_gather, _, members = stars_ref.shape
    n_team = state_ref.shape[0] // out_blocks(state_ref)
    n_blocks = out_blocks(state_ref)
    halves = members // LANES
    n_rows = n_gather * halves

    def spread(r, _):
        block = stars_ref[r]
        for half in range(halves):
            for q in range(7):
                row_ref[q, r * halves + half] = jnp.broadcast_to(
                    block[q : q + 1, half * LANES : (half + 1) * LANES], (8, LANES)
                )
        return 0

    lax.fori_loop(0, n_gather, spread, 0)

    for b in range(n_blocks):
        state = state_ref[b]
        for t in range(1, n_team):
            state = state + state_ref[t * n_blocks + b]
        xi, vi = predict(state[0:3], state[3:6], state[6:9], state[9:12], state[12:13])
        pack = jnp.concatenate([xi, vi, jnp.zeros((2, LANES), jnp.float32)], axis=0)
        col_ref[pl.ds(b * LANES, LANES), :] = pack.T

    groups = 2

    def one_group(g, _):
        ivals = []
        for u in range(groups):
            cols = col_ref[pl.ds((g * groups + u) * 8, 8), :]
            ivals.append([jnp.broadcast_to(cols[:, q : q + 1], (8, LANES)) for q in range(6)])

        def one_row(r, acc):
            px, py, pz, ux, uy, uz, m = [row_ref[q, r] for q in range(7)]
            new = []
            for u in range(groups):
                xi, yi, zi, vxi, vyi, vzi = ivals[u]
                dx, dy, dz = px - xi, py - yi, pz - zi
                dvx, dvy, dvz = ux - vxi, uy - vyi, uz - vzi
                r2 = dx * dx + dy * dy + dz * dz + SOFTEN2
                inv = lax.rsqrt(r2)
                inv2 = inv * inv
                w = m * inv * inv2
                f = w * (inv2 * (dx * dvx + dy * dvy + dz * dvz))
                a = acc[u * 9 : u * 9 + 9]
                new += [
                    a[0] + w * dx, a[1] + w * dy, a[2] + w * dz,
                    a[3] + w * dvx, a[4] + w * dvy, a[5] + w * dvz,
                    a[6] + f * dx, a[7] + f * dy, a[8] + f * dz,
                ]
            return tuple(new)

        acc = lax.fori_loop(0, n_rows, one_row, tuple(jnp.zeros((8, LANES), jnp.float32) for _ in range(9 * groups)), unroll=2)
        for u in range(groups):
            a = acc[u * 9 : u * 9 + 9]
            at = pl.ds((g * groups + u) * 8, 8)
            for q in range(3):
                acc_ref[q, at, :] = a[q]
                acc_ref[3 + q, at, :] = a[3 + q] - 3.0 * a[6 + q]
        return 0

    lax.fori_loop(0, n_blocks * LANES // (8 * groups), one_group, 0)

    for b in range(n_blocks):
        rows = [jnp.sum(acc_ref[q, pl.ds(b * LANES, LANES), :].T, axis=0, keepdims=True) for q in range(6)]
        part = jnp.concatenate(rows + [jnp.zeros((2, LANES), jnp.float32)], axis=0)
        for t in range(n_team):
            out_ref[t * n_blocks + b] = part


def out_blocks(state_ref):
    return N_YLO * N_CORE


def correct_kernel(part_ref, state_ref, phase_ref, force_ref, higher_ref):
    n = part_ref.shape[0]
    n_blocks = N_YLO * N_CORE
    mine = lax.axis_index("y") * N_CORE + lax.axis_index("core")
    total = part_ref[0]
    for k in range(1, n):
        total = total + part_ref[k]
    own = state_ref[mine]
    for t in range(1, n // n_blocks):
        own = own + state_ref[t * n_blocks + mine]
    x0, v0, a0, j0, dt = (own[0:3], own[3:6], own[6:9], own[9:12], own[12:13])
    a1, j1 = (total[0:3], total[3:6])
    v1 = v0 + (a0 + a1) * dt / 2.0 + (j0 - j1) * dt * dt / 12.0
    x1 = x0 + (v0 + v1) * dt / 2.0 + (a0 - a1) * dt * dt / 12.0
    snap = -6.0 * (a0 - a1) - dt * (4.0 * j0 + 2.0 * j1)
    crackle = 12.0 * (a0 - a1) + 6.0 * dt * (j0 + j1)
    phase_ref[...] = jnp.concatenate([x1, v1], 0)
    force_ref[...] = total[0:6]
    higher_ref[...] = jnp.concatenate([snap, crackle], 0)


def shards(sizes, position, velocity, old_accel, old_jerk, mass, elapsed, active_slot, active_owner):
    members = position.shape[1]
    actives = active_slot.shape[0]
    n_gather = sizes["x"] * sizes["z"]
    n_reduce = sizes["team"] * sizes["y"] * sizes["core"]
    n_blocks = sizes["y"] * sizes["core"]
    f32 = jnp.float32
    stars, state = pl.pallas_call(
        pack_kernel,
        out_shape=(
            jax.ShapeDtypeStruct((n_gather, 8, members), f32),
            jax.ShapeDtypeStruct((n_reduce, 16, actives), f32),
        ),
        name="pack",
    )(
        position, velocity, old_accel, old_jerk, mass.reshape(1, members), elapsed.reshape(1, members),
        active_slot.reshape(1, actives), active_owner.reshape(1, actives),
    )
    state = lax.all_to_all(state, REDUCE, 0, 0, tiled=True)
    stars = lax.all_to_all(stars, GATHER, 0, 0, tiled=True)
    n_rows = n_gather * members // LANES
    part = pl.pallas_call(
        force_kernel,
        out_shape=jax.ShapeDtypeStruct((n_reduce, 8, actives), f32),
        scratch_shapes=[
            pltpu.VMEM((7, n_rows, 8, LANES), f32),
            pltpu.VMEM((n_blocks * actives, 8), f32),
            pltpu.VMEM((6, n_blocks * actives, LANES), f32),
        ],
        compiler_params=pltpu.CompilerParams(vmem_limit_bytes=32 * 1024 * 1024),
        name="force",
    )(stars, state)
    part = lax.all_to_all(part, REDUCE, 0, 0, tiled=True)
    out = jax.ShapeDtypeStruct((6, actives), f32)
    return pl.pallas_call(correct_kernel, out_shape=(out, out, out), name="correct")(part, state)


def solution(mesh):
    n_team = mesh.shape["team"]
    fine = Mesh(
        mesh.devices.reshape(n_team, N_X, N_YLO, N_Z, N_CORE), ("team", "x", "y", "z", "core")
    )
    blk = ("x", "y", "z", "core")
    whole = ("team",) + blk
    placed = (
        P(None, whole), P(None, whole), P(None, whole), P(None, whole),
        P(whole), P(whole), P(blk), P(blk),
    )
    return jax.shard_map(
        functools.partial(shards, dict(fine.shape)),
        mesh=fine,
        in_specs=placed,
        out_specs=(P(None, blk), P(None, blk), P(None, blk)),
        check_vma=False,
    )
```

```python
import functools
import jax
import jax.numpy as jnp
from jax import lax
from jax.experimental import pallas as pl
from jax.experimental.pallas import tpu as pltpu
from jax.sharding import Mesh, PartitionSpec as P

SOFTEN2 = 0.0001
N_X, N_YLO, N_Z, N_CORE = 4, 2, 8, 2
LANES = 128
GATHER = ("x", "z")
REDUCE = ("team", "y", "core")
CHUNK = 1024
N_MATRIX = 256
F32 = jnp.float32
BF16 = jnp.bfloat16


def predict(x, v, a, j, h):
    xp = x + h * (v + h * (a / 2.0 + h * j / 6.0))
    vp = v + h * (a + h * j / 2.0)
    return (xp, vp)


def pack_kernel(x_ref, v_ref, a_ref, j_ref, m_ref, h_ref, slot_ref, owner_ref, stars_ref, state_ref):
    x, v, a, j, m, h = (x_ref[...], v_ref[...], a_ref[...], j_ref[...], m_ref[...], h_ref[...])
    xp, vp = predict(x, v, a, j, h)
    members = x.shape[1]
    actives = slot_ref.shape[1]
    star = jnp.concatenate([xp, vp, m, jnp.zeros((1, members), jnp.float32)], axis=0)
    for k in range(stars_ref.shape[0]):
        stars_ref[k] = star
    team = lax.axis_index("team")
    wanted = jnp.where(owner_ref[...] == team, slot_ref[...], -1)
    chooser = (lax.broadcasted_iota(jnp.int32, (members, actives), 0) == wanted).astype(jnp.float32)
    state = jnp.concatenate([x, v, a, j, h, jnp.zeros((3, members), jnp.float32)], axis=0)
    chosen = jnp.dot(state, chooser, precision=lax.Precision.HIGHEST, preferred_element_type=jnp.float32)
    for k in range(state_ref.shape[0]):
        state_ref[k] = chosen


def pieces(value, count):
    out = []
    for _ in range(count - 1):
        piece = value.astype(BF16).astype(F32)
        out.append(piece)
        value = value - piece
    out.append(value.astype(BF16).astype(F32))
    return out


def grid_pieces(value):
    high = jnp.round(value * 64.0) * (1.0 / 64.0)
    first = high.astype(BF16).astype(F32)
    low = value - high
    third = low.astype(BF16).astype(F32)
    return high, low, [first, high - first, third, (low - third).astype(BF16).astype(F32)]


def sum3(rows):
    return rows[0:1] + rows[1:2] + rows[2:3]


def own_terms(high, low, value):
    coarse = sum3(high[0:3] * high[0:3])
    fine = sum3(low[0:3] * (2.0 * high[0:3] + low[0:3]))
    cross = sum3(value[0:3] * value[3:6])
    return pieces(coarse, 3), pieces(fine, 3), pieces(cross, 3)


def star_rows(block):
    n = block.shape[1]
    high, low, p = grid_pieces(block)
    coarse, fine, cross = own_terms(high, low, block)
    one, zero = jnp.ones((1, n), F32), jnp.zeros((1, n), F32)
    stack = []
    for k in range(3):
        stack += [jnp.concatenate([p[k][0:6], coarse[k], fine[k]], 0)] * 4
    stack += [jnp.concatenate([p[3][0:6], one, zero], 0)] * 3
    stack += [jnp.concatenate(cross + [block[0:3], zero, zero], 0)]
    return jnp.concatenate(stack, 0)


def active_rows(pack):
    n = pack.shape[1]
    high, low, p = grid_pieces(pack)
    coarse, fine, cross = own_terms(high, low, pack)
    fine = pieces(sum3(low[0:3] * (2.0 * high[0:3] + low[0:3])) + SOFTEN2, 3)
    zero3, zero, one = jnp.zeros((3, n), F32), jnp.zeros((1, n), F32), jnp.ones((1, n), F32)
    ra, rb, rc = [], [], []
    for k in range(4):
        for l in range(4 if k < 3 else 3):
            is_coarse = k < 2 and l < 2
            unit = one if (l == 0 and k < 3) else zero
            twice = -2.0 * p[l][0:3]
            last = k == 3
            ra.append(jnp.concatenate([twice if is_coarse else zero3, zero3, coarse[l] if last else unit, zero], 0))
            rb.append(jnp.concatenate([zero3 if is_coarse else twice, zero3, fine[l] if last else zero, unit], 0))
            rc.append(jnp.concatenate([-p[l][3:6], -p[l][0:3], cross[l] if last else zero, zero], 0))
    ra.append(jnp.zeros((8, n), F32))
    rb.append(jnp.zeros((8, n), F32))
    rc.append(jnp.concatenate([jnp.ones((3, n), F32), jnp.zeros((5, n), F32)], 0))
    return [jnp.concatenate(rows, 0) for rows in (ra, rb, rc)]


def force_kernel(stars_ref, state_ref, out_ref, met_ref, act_ref):
    n_gather, _, members = stars_ref.shape
    n_blocks = N_YLO * N_CORE
    n_team = state_ref.shape[0] // n_blocks
    n_act = n_blocks * LANES
    per = CHUNK // members
    nm = N_MATRIX
    for b in range(n_blocks):
        state = state_ref[b]
        for t in range(1, n_team):
            state = state + state_ref[t * n_blocks + b]
        xi, vi = predict(state[0:3], state[3:6], state[6:9], state[9:12], state[12:13])
        pack = jnp.concatenate([xi, vi, jnp.zeros((2, LANES), F32)], 0)
        at = b * LANES
        act_ref[:, at : at + LANES] = pack
        ra, rb, rc = active_rows(pack)
        if at < nm:
            met_ref[:, at : at + LANES] = ra.astype(BF16)
            met_ref[:, nm + at : nm + at + LANES] = rb.astype(BF16)
        met_ref[:, 2 * nm + at : 2 * nm + at + LANES] = rc.astype(BF16)

    def one_chunk(c, acc):
        cols, back = [], []
        for q in range(per):
            block = stars_ref[c * per + q]
            cols.append(star_rows(block).T)
            heavy = jnp.concatenate([block[0:6] * block[6:7], block[6:8]], 0)
            back.append(jnp.concatenate(pieces(heavy, 3), 0))
        cols = jnp.concatenate(cols, 0)
        back = jnp.concatenate(back, 1).astype(BF16)
        feats = cols.astype(BF16)
        two = jnp.dot(feats, met_ref[:, : 2 * nm], preferred_element_type=F32)
        cross = jnp.dot(feats, met_ref[:, 2 * nm :], preferred_element_type=F32)
        d = [cols[:, 123 + q : 124 + q] - act_ref[q : q + 1, nm:] for q in range(3)]
        r2 = jnp.concatenate(
            [two[:, :nm] + two[:, nm:], d[0] * d[0] + d[1] * d[1] + d[2] * d[2] + SOFTEN2], 1
        )
        inv = lax.rsqrt(r2)
        inv2 = inv * inv
        w = inv * inv2
        u = w * inv2 * cross
        sums = []
        for value in (w, u):
            upper = value.astype(BF16)
            lower = (value - upper.astype(F32)).astype(BF16)
            sums.append(
                jnp.dot(back, upper, preferred_element_type=F32)
                + jnp.dot(back, lower, preferred_element_type=F32)
            )
        return acc[0] + sums[0], acc[1] + sums[1]

    zero = jnp.zeros((24, n_act), F32)
    sw, su = lax.fori_loop(0, n_gather * members // CHUNK, one_chunk, (zero, zero), unroll=2)
    sw = sw[16:24] + sw[8:16] + sw[0:8]
    su = su[16:24] + su[8:16] + su[0:8]
    xi, vi = act_ref[0:3, :], act_ref[3:6, :]
    a = sw[0:3] - xi * sw[6:7]
    j = (sw[3:6] - vi * sw[6:7]) - 3.0 * (su[0:3] - xi * su[6:7])
    part = jnp.concatenate([a, j, jnp.zeros((2, n_act), F32)], 0)
    for b in range(n_blocks):
        for t in range(n_team):
            out_ref[t * n_blocks + b] = part[:, b * LANES : (b + 1) * LANES]


def correct_kernel(part_ref, state_ref, phase_ref, force_ref, higher_ref):
    n = part_ref.shape[0]
    n_blocks = N_YLO * N_CORE
    mine = lax.axis_index("y") * N_CORE + lax.axis_index("core")
    total = part_ref[0]
    for k in range(1, n):
        total = total + part_ref[k]
    own = state_ref[mine]
    for t in range(1, n // n_blocks):
        own = own + state_ref[t * n_blocks + mine]
    x0, v0, a0, j0, dt = (own[0:3], own[3:6], own[6:9], own[9:12], own[12:13])
    a1, j1 = (total[0:3], total[3:6])
    v1 = v0 + (a0 + a1) * dt / 2.0 + (j0 - j1) * dt * dt / 12.0
    x1 = x0 + (v0 + v1) * dt / 2.0 + (a0 - a1) * dt * dt / 12.0
    snap = -6.0 * (a0 - a1) - dt * (4.0 * j0 + 2.0 * j1)
    crackle = 12.0 * (a0 - a1) + 6.0 * dt * (j0 + j1)
    phase_ref[...] = jnp.concatenate([x1, v1], 0)
    force_ref[...] = total[0:6]
    higher_ref[...] = jnp.concatenate([snap, crackle], 0)


def shards(sizes, position, velocity, old_accel, old_jerk, mass, elapsed, active_slot, active_owner):
    members = position.shape[1]
    actives = active_slot.shape[0]
    n_gather = sizes["x"] * sizes["z"]
    n_reduce = sizes["team"] * sizes["y"] * sizes["core"]
    n_blocks = sizes["y"] * sizes["core"]
    stars, state = pl.pallas_call(
        pack_kernel,
        out_shape=(
            jax.ShapeDtypeStruct((n_gather, 8, members), F32),
            jax.ShapeDtypeStruct((n_reduce, 16, actives), F32),
        ),
        name="pack",
    )(
        position, velocity, old_accel, old_jerk, mass.reshape(1, members), elapsed.reshape(1, members),
        active_slot.reshape(1, actives), active_owner.reshape(1, actives),
    )
    state = lax.all_to_all(state, REDUCE, 0, 0, tiled=True)
    stars = lax.all_to_all(stars, GATHER, 0, 0, tiled=True)
    part = pl.pallas_call(
        force_kernel,
        out_shape=jax.ShapeDtypeStruct((n_reduce, 8, actives), F32),
        scratch_shapes=[
            pltpu.VMEM((LANES, 2 * N_MATRIX + n_blocks * actives), BF16),
            pltpu.VMEM((8, n_blocks * actives), F32),
        ],
        compiler_params=pltpu.CompilerParams(vmem_limit_bytes=48 * 1024 * 1024),
        name="force",
    )(stars, state)
    part = lax.all_to_all(part, REDUCE, 0, 0, tiled=True)
    out = jax.ShapeDtypeStruct((6, actives), F32)
    return pl.pallas_call(correct_kernel, out_shape=(out, out, out), name="correct")(part, state)


def solution(mesh):
    n_team = mesh.shape["team"]
    fine = Mesh(
        mesh.devices.reshape(n_team, N_X, N_YLO, N_Z, N_CORE), ("team", "x", "y", "z", "core")
    )
    blk = ("x", "y", "z", "core")
    whole = ("team",) + blk
    placed = (
        P(None, whole), P(None, whole), P(None, whole), P(None, whole),
        P(whole), P(whole), P(blk), P(blk),
    )
    return jax.shard_map(
        functools.partial(shards, dict(fine.shape)),
        mesh=fine,
        in_specs=placed,
        out_specs=(P(None, blk), P(None, blk), P(None, blk)),
        check_vma=False,
    )
```

```python
import functools
import jax
import jax.numpy as jnp
from jax import lax
from jax.experimental import pallas as pl
from jax.experimental.pallas import tpu as pltpu
from jax.sharding import Mesh, PartitionSpec as P

SOFTEN2 = 0.0001
N_X, N_YLO, N_Z, N_CORE = 4, 2, 8, 2
LANES = 128
GATHER = ("x", "z")
REDUCE = ("team", "y", "core")
SIDE = 256
CYCLE = 4
F32 = jnp.float32
BF16 = jnp.bfloat16


def predict(x, v, a, j, h):
    xp = x + h * (v + h * (a / 2.0 + h * j / 6.0))
    vp = v + h * (a + h * j / 2.0)
    return (xp, vp)


def pack_kernel(x_ref, v_ref, a_ref, j_ref, m_ref, h_ref, slot_ref, owner_ref, stars_ref, state_ref):
    x, v, a, j, m, h = (x_ref[...], v_ref[...], a_ref[...], j_ref[...], m_ref[...], h_ref[...])
    xp, vp = predict(x, v, a, j, h)
    members = x.shape[1]
    actives = slot_ref.shape[1]
    star = jnp.concatenate([xp, vp, m, jnp.zeros((1, members), jnp.float32)], axis=0)
    for k in range(stars_ref.shape[0]):
        stars_ref[k] = star
    team = lax.axis_index("team")
    wanted = jnp.where(owner_ref[...] == team, slot_ref[...], -1)
    chooser = (lax.broadcasted_iota(jnp.int32, (members, actives), 0) == wanted).astype(jnp.float32)
    state = jnp.concatenate([x, v, a, j, h, jnp.zeros((3, members), jnp.float32)], axis=0)
    chosen = jnp.dot(state, chooser, precision=lax.Precision.HIGHEST, preferred_element_type=jnp.float32)
    for k in range(state_ref.shape[0]):
        state_ref[k] = chosen


def rounded(value):
    return value.astype(BF16).astype(F32)


def pieces(value):
    first = rounded(value)
    rest = value - first
    second = rounded(rest)
    return [first, second, rest - second]


def grid_pieces(value):
    high = jnp.round(value * 128.0) * (1.0 / 128.0)
    first = rounded(high)
    low = value - high
    third = rounded(low)
    return high, low, [first, high - first, third, low - third]


def star_rows(block):
    row = lax.broadcasted_iota(jnp.int32, block.shape, 0)

    def roll(value, shift):
        return pltpu.roll(value, shift, 0)

    moving = jnp.where(row < 6, block, 0.0)
    high, low, p = grid_pieces(moving)
    square = high * high
    twice = low * (2.0 * high + low)
    coarse = roll(square, 6) + roll(square, 5) + roll(square, 4)
    fine = roll(twice, 7) + roll(twice, 6) + roll(twice, 5)
    own = pieces(jnp.where(row == 6, coarse, jnp.where(row == 7, fine, 0.0)))
    both = moving * roll(moving, 5)
    cross = both + roll(both, 7) + roll(both, 6)
    c = pieces(jnp.broadcast_to(cross[0:1], cross.shape))
    last = jnp.where(row < 6, roll(block, 3), 0.0)
    for k in range(3):
        last = jnp.where(row == k, c[k], last)
    stack = []
    for k in range(3):
        stack += [p[k] + own[k]] * 4
    stack += [jnp.where(row == 6, 1.0, p[3])] * 3 + [last]
    return jnp.concatenate(stack, 0)


def sum3(rows):
    return rows[0:1] + rows[1:2] + rows[2:3]


def active_rows(pack):
    n = pack.shape[1]
    high, low, p = grid_pieces(pack)
    coarse = pieces(sum3(high[0:3] * high[0:3]))
    fine = pieces(sum3(low[0:3] * (2.0 * high[0:3] + low[0:3])) + SOFTEN2)
    cross = pieces(sum3(pack[0:3] * pack[3:6]))
    zero3, zero, one = jnp.zeros((3, n), F32), jnp.zeros((1, n), F32), jnp.ones((1, n), F32)
    ra, rb, rc = [], [], []
    for k in range(4):
        for l in range(4 if k < 3 else 3):
            is_coarse = k < 2 and l < 2
            unit = one if (l == 0 and k < 3) else zero
            twice = -2.0 * p[l][0:3]
            last = k == 3
            ra.append(jnp.concatenate([twice if is_coarse else zero3, zero3, coarse[l] if last else unit, zero], 0))
            rb.append(jnp.concatenate([zero3 if is_coarse else twice, zero3, fine[l] if last else zero, unit], 0))
            rc.append(jnp.concatenate([-p[l][3:6], -p[l][0:3], cross[l] if last else zero, zero], 0))
    ra.append(jnp.zeros((8, n), F32))
    rb.append(jnp.zeros((8, n), F32))
    rc.append(jnp.concatenate([jnp.ones((3, n), F32), jnp.zeros((5, n), F32)], 0))
    return [jnp.concatenate(rows, 0) for rows in (ra, rb, rc)]


def heavy_rows(block):
    row = lax.broadcasted_iota(jnp.int32, block.shape, 0)
    heavy = jnp.where(row == 6, block, block * block[6:7])
    return jnp.concatenate(pieces(heavy), 0).astype(BF16)


def force_kernel(stars_ref, state_ref, out_ref, met_ref, act_ref, sum_ref, feat_ref, prod_ref, weight_ref, col_ref):
    n_tiles = stars_ref.shape[0]
    n_blocks = N_YLO * N_CORE
    n_team = state_ref.shape[0] // n_blocks
    n_act = n_blocks * LANES
    sides = range(0, n_act, SIDE)

    for b in range(n_blocks):
        state = state_ref[b]
        for t in range(1, n_team):
            state = state + state_ref[t * n_blocks + b]
        xi, vi = predict(state[0:3], state[3:6], state[6:9], state[9:12], state[12:13])
        pack = jnp.concatenate([xi, vi, jnp.zeros((2, LANES), F32)], 0)
        at = b * LANES
        act_ref[:, at : at + LANES] = pack
        for k, rows in enumerate(active_rows(pack)):
            met_ref[:, k * n_act + at : k * n_act + at + LANES] = rows.astype(BF16)

    def on_matrix(tile, side):
        return side < n_act // 2 or tile % CYCLE != CYCLE - 1

    def prepare(t, tile):
        cols = star_rows(stars_ref[t]).T
        feat_ref[...] = cols.astype(BF16)
        if not on_matrix(tile, n_act - 1):
            col_ref[...] = cols

    def products(side, tile):
        for k in (0, 1, 2) if on_matrix(tile, side) else (2,):
            at = k * n_act + side
            prod_ref[:, at : at + SIDE] = jnp.dot(
                feat_ref[...], met_ref[:, at : at + SIDE], preferred_element_type=F32
            )

    def weights(side, tile):
        cross = prod_ref[:, 2 * n_act + side : 2 * n_act + side + SIDE]
        if on_matrix(tile, side):
            r2 = prod_ref[:, side : side + SIDE] + prod_ref[:, n_act + side : n_act + side + SIDE]
        else:
            cols = col_ref[...]
            d = [cols[:, 123 + q : 124 + q] - act_ref[q : q + 1, side : side + SIDE] for q in range(3)]
            r2 = d[0] * d[0] + d[1] * d[1] + d[2] * d[2] + SOFTEN2
        inv = lax.rsqrt(r2)
        inv2 = inv * inv
        w = inv * inv2
        u = w * inv2 * cross
        for k, value in enumerate((w, u)):
            upper = value.astype(BF16)
            at = 2 * k * n_act + side
            weight_ref[:, at : at + SIDE] = upper
            at = at + n_act
            weight_ref[:, at : at + SIDE] = (value - upper.astype(F32)).astype(BF16)

    def add_up(heavy, side):
        for k in range(2):
            at = 2 * k * n_act + side
            upper, lower = weight_ref[:, at : at + SIDE], weight_ref[:, at + n_act : at + n_act + SIDE]
            part = jnp.dot(heavy, upper, preferred_element_type=F32) + jnp.dot(
                heavy, lower, preferred_element_type=F32
            )
            at = k * n_act + side
            sum_ref[:, at : at + SIDE] = sum_ref[:, at : at + SIDE] + part

    sum_ref[...] = jnp.zeros_like(sum_ref)
    prepare(0, 0)
    for side in sides:
        products(side, 0)
    prepare(1, 1)

    def one_cycle(c, _):
        for tile in range(CYCLE):
            t = c * CYCLE + tile
            heavy = heavy_rows(stars_ref[t])
            for side in sides:
                weights(side, tile)
                products(side, tile + 1)
                add_up(heavy, side)
            prepare(jnp.minimum(t + 2, n_tiles - 1), tile + 2)
        return 0

    lax.fori_loop(0, n_tiles // CYCLE, one_cycle, 0, unroll=2)
    sums = sum_ref[16:24, :] + sum_ref[8:16, :] + sum_ref[0:8, :]
    sw, su = sums[:, :n_act], sums[:, n_act:]
    xi, vi = act_ref[0:3, :], act_ref[3:6, :]
    a = sw[0:3] - xi * sw[6:7]
    j = (sw[3:6] - vi * sw[6:7]) - 3.0 * (su[0:3] - xi * su[6:7])
    part = jnp.concatenate([a, j, jnp.zeros((2, n_act), F32)], 0)
    for b in range(n_blocks):
        for t in range(n_team):
            out_ref[t * n_blocks + b] = part[:, b * LANES : (b + 1) * LANES]


def correct_kernel(part_ref, state_ref, phase_ref, force_ref, higher_ref):
    n = part_ref.shape[0]
    n_blocks = N_YLO * N_CORE
    mine = lax.axis_index("y") * N_CORE + lax.axis_index("core")
    total = part_ref[0]
    for k in range(1, n):
        total = total + part_ref[k]
    own = state_ref[mine]
    for t in range(1, n // n_blocks):
        own = own + state_ref[t * n_blocks + mine]
    x0, v0, a0, j0, dt = (own[0:3], own[3:6], own[6:9], own[9:12], own[12:13])
    a1, j1 = (total[0:3], total[3:6])
    v1 = v0 + (a0 + a1) * dt / 2.0 + (j0 - j1) * dt * dt / 12.0
    x1 = x0 + (v0 + v1) * dt / 2.0 + (a0 - a1) * dt * dt / 12.0
    snap = -6.0 * (a0 - a1) - dt * (4.0 * j0 + 2.0 * j1)
    crackle = 12.0 * (a0 - a1) + 6.0 * dt * (j0 + j1)
    phase_ref[...] = jnp.concatenate([x1, v1], 0)
    force_ref[...] = total[0:6]
    higher_ref[...] = jnp.concatenate([snap, crackle], 0)


def shards(sizes, position, velocity, old_accel, old_jerk, mass, elapsed, active_slot, active_owner):
    members = position.shape[1]
    actives = active_slot.shape[0]
    n_gather = sizes["x"] * sizes["z"]
    n_reduce = sizes["team"] * sizes["y"] * sizes["core"]
    n_blocks = sizes["y"] * sizes["core"]
    stars, state = pl.pallas_call(
        pack_kernel,
        out_shape=(
            jax.ShapeDtypeStruct((n_gather, 8, members), F32),
            jax.ShapeDtypeStruct((n_reduce, 16, actives), F32),
        ),
        name="pack",
    )(
        position, velocity, old_accel, old_jerk, mass.reshape(1, members), elapsed.reshape(1, members),
        active_slot.reshape(1, actives), active_owner.reshape(1, actives),
    )
    state = lax.all_to_all(state, REDUCE, 0, 0, tiled=True)
    stars = lax.all_to_all(stars, GATHER, 0, 0, tiled=True)
    n_act = n_blocks * actives
    part = pl.pallas_call(
        force_kernel,
        out_shape=jax.ShapeDtypeStruct((n_reduce, 8, actives), F32),
        scratch_shapes=[
            pltpu.VMEM((LANES, 3 * n_act), BF16),
            pltpu.VMEM((8, n_act), F32),
            pltpu.VMEM((24, 2 * n_act), F32),
            pltpu.VMEM((members, LANES), BF16),
            pltpu.VMEM((members, 3 * n_act), F32),
            pltpu.VMEM((members, 4 * n_act), BF16),
            pltpu.VMEM((members, LANES), F32),
        ],
        compiler_params=pltpu.CompilerParams(vmem_limit_bytes=48 * 1024 * 1024),
        name="force",
    )(stars, state)
    part = lax.all_to_all(part, REDUCE, 0, 0, tiled=True)
    out = jax.ShapeDtypeStruct((6, actives), F32)
    return pl.pallas_call(correct_kernel, out_shape=(out, out, out), name="correct")(part, state)


def solution(mesh):
    n_team = mesh.shape["team"]
    fine = Mesh(
        mesh.devices.reshape(n_team, N_X, N_YLO, N_Z, N_CORE), ("team", "x", "y", "z", "core")
    )
    blk = ("x", "y", "z", "core")
    whole = ("team",) + blk
    placed = (
        P(None, whole), P(None, whole), P(None, whole), P(None, whole),
        P(whole), P(whole), P(blk), P(blk),
    )
    return jax.shard_map(
        functools.partial(shards, dict(fine.shape)),
        mesh=fine,
        in_specs=placed,
        out_specs=(P(None, blk), P(None, blk), P(None, blk)),
        check_vma=False,
    )
```

```python
import functools
import jax
import jax.numpy as jnp
from jax import lax
from jax.experimental import pallas as pl
from jax.experimental.pallas import tpu as pltpu
from jax.sharding import Mesh, PartitionSpec as P

SOFTEN2 = 0.0001
N_X, N_YLO, N_Z, N_CORE = 4, 2, 8, 2
LANES = 128
GATHER = ("x", "z")
REDUCE = ("team", "y", "core")
SIDE = 256
CYCLE = 4
F32 = jnp.float32
BF16 = jnp.bfloat16


def predict(x, v, a, j, h):
    xp = x + h * (v + h * (a / 2.0 + h * j / 6.0))
    vp = v + h * (a + h * j / 2.0)
    return (xp, vp)


def state_kernel(x_ref, v_ref, a_ref, j_ref, h_ref, slot_ref, owner_ref, state_ref):
    members, actives = x_ref.shape[1], slot_ref.shape[1]
    team = lax.axis_index("team")
    wanted = jnp.where(owner_ref[...] == team, slot_ref[...], -1)
    chooser = (lax.broadcasted_iota(jnp.int32, (members, actives), 0) == wanted).astype(F32)
    state = jnp.concatenate(
        [x_ref[...], v_ref[...], a_ref[...], j_ref[...], h_ref[...], jnp.zeros((3, members), F32)], axis=0
    )
    chosen = jnp.dot(state, chooser, precision=lax.Precision.HIGHEST, preferred_element_type=F32)
    for k in range(state_ref.shape[0]):
        state_ref[k] = chosen


def star_kernel(x_ref, v_ref, a_ref, j_ref, m_ref, h_ref, stars_ref):
    xp, vp = predict(x_ref[...], v_ref[...], a_ref[...], j_ref[...], h_ref[...])
    rows = [value[q : q + 1] for value in (xp, vp) for q in range(3)] + [m_ref[...]]
    star = jnp.concatenate(rows, axis=1)
    for k in range(stars_ref.shape[0]):
        stars_ref[k] = star


def rounded(value):
    return value.astype(BF16).astype(F32)


def pieces(value):
    first = rounded(value)
    rest = value - first
    second = rounded(rest)
    return [first, second, rest - second]


def grid_pieces(value):
    high = jnp.round(value * 128.0) * (1.0 / 128.0)
    first = rounded(high)
    low = value - high
    third = rounded(low)
    return high, low, [first, high - first, third, low - third]


def star_rows(block):
    row = lax.broadcasted_iota(jnp.int32, block.shape, 0)

    def roll(value, shift):
        return pltpu.roll(value, shift, 0)

    moving = jnp.where(row < 6, block, 0.0)
    high, low, p = grid_pieces(moving)
    square = high * high
    twice = low * (2.0 * high + low)
    coarse = roll(square, 6) + roll(square, 5) + roll(square, 4)
    fine = roll(twice, 7) + roll(twice, 6) + roll(twice, 5)
    own = pieces(jnp.where(row == 6, coarse, jnp.where(row == 7, fine, 0.0)))
    both = moving * roll(moving, 5)
    cross = both + roll(both, 7) + roll(both, 6)
    c = pieces(jnp.broadcast_to(cross[0:1], cross.shape))
    last = jnp.where(row < 6, roll(block, 3), 0.0)
    for k in range(3):
        last = jnp.where(row == k, c[k], last)
    stack = []
    for k in range(3):
        stack += [p[k] + own[k]] * 4
    stack += [jnp.where(row == 6, 1.0, p[3])] * 3 + [last]
    return jnp.concatenate(stack, 0)


def sum3(rows):
    return rows[0:1] + rows[1:2] + rows[2:3]


def active_rows(pack):
    n = pack.shape[1]
    high, low, p = grid_pieces(pack)
    coarse = pieces(sum3(high[0:3] * high[0:3]))
    fine = pieces(sum3(low[0:3] * (2.0 * high[0:3] + low[0:3])) + SOFTEN2)
    cross = pieces(sum3(pack[0:3] * pack[3:6]))
    zero3, zero, one = jnp.zeros((3, n), F32), jnp.zeros((1, n), F32), jnp.ones((1, n), F32)
    ra, rb, rc = [], [], []
    for k in range(4):
        for l in range(4 if k < 3 else 3):
            is_coarse = k < 2 and l < 2
            unit = one if (l == 0 and k < 3) else zero
            twice = -2.0 * p[l][0:3]
            last = k == 3
            ra.append(jnp.concatenate([twice if is_coarse else zero3, zero3, coarse[l] if last else unit, zero], 0))
            rb.append(jnp.concatenate([zero3 if is_coarse else twice, zero3, fine[l] if last else zero, unit], 0))
            rc.append(jnp.concatenate([-p[l][3:6], -p[l][0:3], cross[l] if last else zero, zero], 0))
    ra.append(jnp.zeros((8, n), F32))
    rb.append(jnp.zeros((8, n), F32))
    rc.append(jnp.concatenate([jnp.ones((3, n), F32), jnp.zeros((5, n), F32)], 0))
    return [jnp.concatenate(rows, 0) for rows in (ra, rb, rc)]


def heavy_rows(block):
    row = lax.broadcasted_iota(jnp.int32, block.shape, 0)
    heavy = jnp.where(row == 6, block, block * block[6:7])
    return jnp.concatenate(pieces(heavy), 0).astype(BF16)


def force_kernel(stars_ref, state_ref, out_ref, met_ref, act_ref, sum_ref, feat_ref, prod_ref, weight_ref, col_ref):
    n_tiles = stars_ref.shape[0]
    n_blocks = N_YLO * N_CORE
    n_team = state_ref.shape[0] // n_blocks
    n_act = n_blocks * LANES
    sides = range(0, n_act, SIDE)

    for b in range(n_blocks):
        state = state_ref[b]
        for t in range(1, n_team):
            state = state + state_ref[t * n_blocks + b]
        xi, vi = predict(state[0:3], state[3:6], state[6:9], state[9:12], state[12:13])
        pack = jnp.concatenate([xi, vi, jnp.zeros((2, LANES), F32)], 0)
        at = b * LANES
        act_ref[:, at : at + LANES] = pack
        for k, rows in enumerate(active_rows(pack)):
            met_ref[:, k * n_act + at : k * n_act + at + LANES] = rows.astype(BF16)

    def block_of(t):
        line = stars_ref[t]
        members = line.shape[1] // 7
        rows = [line[:, q * members : (q + 1) * members] for q in range(7)]
        return jnp.concatenate(rows + [jnp.zeros((1, members), F32)], 0)

    def on_matrix(tile, side):
        return side < n_act // 2 or tile % CYCLE != CYCLE - 1

    def prepare(t, tile):
        cols = star_rows(block_of(t)).T
        feat_ref[...] = cols.astype(BF16)
        if not on_matrix(tile, n_act - 1):
            col_ref[...] = cols

    def products(side, tile):
        for k in (0, 1, 2) if on_matrix(tile, side) else (2,):
            at = k * n_act + side
            prod_ref[:, at : at + SIDE] = jnp.dot(
                feat_ref[...], met_ref[:, at : at + SIDE], preferred_element_type=F32
            )

    def weights(side, tile):
        cross = prod_ref[:, 2 * n_act + side : 2 * n_act + side + SIDE]
        if on_matrix(tile, side):
            r2 = prod_ref[:, side : side + SIDE] + prod_ref[:, n_act + side : n_act + side + SIDE]
        else:
            cols = col_ref[...]
            d = [cols[:, 123 + q : 124 + q] - act_ref[q : q + 1, side : side + SIDE] for q in range(3)]
            r2 = d[0] * d[0] + d[1] * d[1] + d[2] * d[2] + SOFTEN2
        inv = lax.rsqrt(r2)
        inv2 = inv * inv
        w = inv * inv2
        u = w * inv2 * cross
        for k, value in enumerate((w, u)):
            upper = value.astype(BF16)
            at = 2 * k * n_act + side
            weight_ref[:, at : at + SIDE] = upper
            at = at + n_act
            weight_ref[:, at : at + SIDE] = (value - upper.astype(F32)).astype(BF16)

    def add_up(heavy, side):
        for k in range(2):
            at = 2 * k * n_act + side
            upper, lower = weight_ref[:, at : at + SIDE], weight_ref[:, at + n_act : at + n_act + SIDE]
            part = jnp.dot(heavy, upper, preferred_element_type=F32) + jnp.dot(
                heavy, lower, preferred_element_type=F32
            )
            at = k * n_act + side
            sum_ref[:, at : at + SIDE] = sum_ref[:, at : at + SIDE] + part

    sum_ref[...] = jnp.zeros_like(sum_ref)
    prepare(0, 0)
    for side in sides:
        products(side, 0)
    prepare(1, 1)

    def one_cycle(c, _):
        for tile in range(CYCLE):
            t = c * CYCLE + tile
            heavy = heavy_rows(block_of(t))
            for side in sides:
                weights(side, tile)
                products(side, tile + 1)
                add_up(heavy, side)
            prepare(jnp.minimum(t + 2, n_tiles - 1), tile + 2)
        return 0

    lax.fori_loop(0, n_tiles // CYCLE, one_cycle, 0, unroll=2)
    sums = sum_ref[16:24, :] + sum_ref[8:16, :] + sum_ref[0:8, :]
    sw, su = sums[:, :n_act], sums[:, n_act:]
    xi, vi = act_ref[0:3, :], act_ref[3:6, :]
    a = sw[0:3] - xi * sw[6:7]
    j = (sw[3:6] - vi * sw[6:7]) - 3.0 * (su[0:3] - xi * su[6:7])
    part = jnp.concatenate([a, j, jnp.zeros((2, n_act), F32)], 0)
    for b in range(n_blocks):
        for t in range(n_team):
            out_ref[t * n_blocks + b] = part[:, b * LANES : (b + 1) * LANES]


def correct_kernel(part_ref, state_ref, phase_ref, force_ref, higher_ref):
    n = part_ref.shape[0]
    n_blocks = N_YLO * N_CORE
    mine = lax.axis_index("y") * N_CORE + lax.axis_index("core")
    total = part_ref[0]
    for k in range(1, n):
        total = total + part_ref[k]
    own = state_ref[mine]
    for t in range(1, n // n_blocks):
        own = own + state_ref[t * n_blocks + mine]
    x0, v0, a0, j0, dt = (own[0:3], own[3:6], own[6:9], own[9:12], own[12:13])
    a1, j1 = (total[0:3], total[3:6])
    v1 = v0 + (a0 + a1) * dt / 2.0 + (j0 - j1) * dt * dt / 12.0
    x1 = x0 + (v0 + v1) * dt / 2.0 + (a0 - a1) * dt * dt / 12.0
    snap = -6.0 * (a0 - a1) - dt * (4.0 * j0 + 2.0 * j1)
    crackle = 12.0 * (a0 - a1) + 6.0 * dt * (j0 + j1)
    phase_ref[...] = jnp.concatenate([x1, v1], 0)
    force_ref[...] = total[0:6]
    higher_ref[...] = jnp.concatenate([snap, crackle], 0)


def shards(sizes, position, velocity, old_accel, old_jerk, mass, elapsed, active_slot, active_owner):
    members = position.shape[1]
    actives = active_slot.shape[0]
    n_gather = sizes["x"] * sizes["z"]
    n_reduce = sizes["team"] * sizes["y"] * sizes["core"]
    n_blocks = sizes["y"] * sizes["core"]
    elapsed = elapsed.reshape(1, members)
    state = pl.pallas_call(
        state_kernel, out_shape=jax.ShapeDtypeStruct((n_reduce, 16, actives), F32), name="state"
    )(
        position, velocity, old_accel, old_jerk, elapsed,
        active_slot.reshape(1, actives), active_owner.reshape(1, actives),
    )
    stars = pl.pallas_call(
        star_kernel, out_shape=jax.ShapeDtypeStruct((n_gather, 1, 7 * members), F32), name="stars"
    )(position, velocity, old_accel, old_jerk, mass.reshape(1, members), elapsed)
    state = lax.all_to_all(state, REDUCE, 0, 0, tiled=True)
    stars = lax.all_to_all(stars, GATHER, 0, 0, tiled=True)
    n_act = n_blocks * actives
    part = pl.pallas_call(
        force_kernel,
        out_shape=jax.ShapeDtypeStruct((n_reduce, 8, actives), F32),
        scratch_shapes=[
            pltpu.VMEM((LANES, 3 * n_act), BF16),
            pltpu.VMEM((8, n_act), F32),
            pltpu.VMEM((24, 2 * n_act), F32),
            pltpu.VMEM((members, LANES), BF16),
            pltpu.VMEM((members, 3 * n_act), F32),
            pltpu.VMEM((members, 4 * n_act), BF16),
            pltpu.VMEM((members, LANES), F32),
        ],
        compiler_params=pltpu.CompilerParams(vmem_limit_bytes=48 * 1024 * 1024),
        name="force",
    )(stars, state)
    part = lax.all_to_all(part, REDUCE, 0, 0, tiled=True)
    out = jax.ShapeDtypeStruct((6, actives), F32)
    return pl.pallas_call(correct_kernel, out_shape=(out, out, out), name="correct")(part, state)


def solution(mesh):
    n_team = mesh.shape["team"]
    fine = Mesh(
        mesh.devices.reshape(n_team, N_X, N_YLO, N_Z, N_CORE), ("team", "x", "y", "z", "core")
    )
    blk = ("x", "y", "z", "core")
    whole = ("team",) + blk
    placed = (
        P(None, whole), P(None, whole), P(None, whole), P(None, whole),
        P(whole), P(whole), P(blk), P(blk),
    )
    return jax.shard_map(
        functools.partial(shards, dict(fine.shape)),
        mesh=fine,
        in_specs=placed,
        out_specs=(P(None, blk), P(None, blk), P(None, blk)),
        check_vma=False,
    )
```

```python
import functools
import jax
import jax.numpy as jnp
from jax import lax
from jax.experimental import pallas as pl
from jax.experimental.pallas import tpu as pltpu
from jax.sharding import Mesh, PartitionSpec as P

SOFTEN2 = 0.0001
N_X, N_YLO, N_Z, N_CORE = 4, 2, 8, 2
LANES = 128
GATHER = ("x", "z")
REDUCE = ("team", "y", "core")
SIDE = 256
CYCLE = 4
SMALL = 4 * 1024 * 1024
F32 = jnp.float32
BF16 = jnp.bfloat16


def predict(x, v, a, j, h):
    xp = x + h * (v + h * (a / 2.0 + h * j / 6.0))
    vp = v + h * (a + h * j / 2.0)
    return (xp, vp)


def state_kernel(x_ref, v_ref, a_ref, j_ref, h_ref, slot_ref, owner_ref, state_ref):
    members, actives = x_ref.shape[1], slot_ref.shape[1]
    team = lax.axis_index("team")
    wanted = jnp.where(owner_ref[...] == team, slot_ref[...], -1)
    chooser = (lax.broadcasted_iota(jnp.int32, (members, actives), 0) == wanted).astype(F32)
    state = jnp.concatenate(
        [x_ref[...], v_ref[...], a_ref[...], j_ref[...], h_ref[...], jnp.zeros((3, members), F32)], axis=0
    )
    chosen = jnp.dot(state, chooser, precision=lax.Precision.HIGHEST, preferred_element_type=F32)
    for k in range(state_ref.shape[0]):
        state_ref[k] = chosen


def star_kernel(x_ref, v_ref, a_ref, j_ref, m_ref, h_ref, stars_ref):
    xp, vp = predict(x_ref[...], v_ref[...], a_ref[...], j_ref[...], h_ref[...])
    rows = [value[q : q + 1] for value in (xp, vp) for q in range(3)] + [m_ref[...]]
    star = jnp.concatenate(rows, axis=1)
    for k in range(stars_ref.shape[0]):
        stars_ref[k] = star


def rounded(value):
    return value.astype(BF16).astype(F32)


def pieces(value):
    first = rounded(value)
    rest = value - first
    second = rounded(rest)
    return [first, second, rest - second]


def grid_pieces(value):
    high = jnp.round(value * 128.0) * (1.0 / 128.0)
    first = rounded(high)
    low = value - high
    third = rounded(low)
    return high, low, [first, high - first, third, low - third]


def star_rows(block):
    row = lax.broadcasted_iota(jnp.int32, block.shape, 0)

    def roll(value, shift):
        return pltpu.roll(value, shift, 0)

    moving = jnp.where(row < 6, block, 0.0)
    high, low, p = grid_pieces(moving)
    square = high * high
    twice = low * (2.0 * high + low)
    coarse = roll(square, 6) + roll(square, 5) + roll(square, 4)
    fine = roll(twice, 7) + roll(twice, 6) + roll(twice, 5)
    own = pieces(jnp.where(row == 6, coarse, jnp.where(row == 7, fine, 0.0)))
    both = moving * roll(moving, 5)
    cross = both + roll(both, 7) + roll(both, 6)
    c = pieces(jnp.broadcast_to(cross[0:1], cross.shape))
    last = jnp.where(row < 6, roll(block, 3), 0.0)
    for k in range(3):
        last = jnp.where(row == k, c[k], last)
    stack = []
    for k in range(3):
        stack += [p[k] + own[k]] * 4
    stack += [jnp.where(row == 6, 1.0, p[3])] * 3 + [last]
    return jnp.concatenate(stack, 0)


def sum3(rows):
    return rows[0:1] + rows[1:2] + rows[2:3]


def active_rows(pack):
    n = pack.shape[1]
    high, low, p = grid_pieces(pack)
    coarse = pieces(sum3(high[0:3] * high[0:3]))
    fine = pieces(sum3(low[0:3] * (2.0 * high[0:3] + low[0:3])) + SOFTEN2)
    cross = pieces(sum3(pack[0:3] * pack[3:6]))
    zero3, zero, one = jnp.zeros((3, n), F32), jnp.zeros((1, n), F32), jnp.ones((1, n), F32)
    ra, rb, rc = [], [], []
    for k in range(4):
        for l in range(4 if k < 3 else 3):
            is_coarse = k < 2 and l < 2
            unit = one if (l == 0 and k < 3) else zero
            twice = -2.0 * p[l][0:3]
            last = k == 3
            ra.append(jnp.concatenate([twice if is_coarse else zero3, zero3, coarse[l] if last else unit, zero], 0))
            rb.append(jnp.concatenate([zero3 if is_coarse else twice, zero3, fine[l] if last else zero, unit], 0))
            rc.append(jnp.concatenate([-p[l][3:6], -p[l][0:3], cross[l] if last else zero, zero], 0))
    ra.append(jnp.zeros((8, n), F32))
    rb.append(jnp.zeros((8, n), F32))
    rc.append(jnp.concatenate([jnp.ones((3, n), F32), jnp.zeros((5, n), F32)], 0))
    return [jnp.concatenate(rows, 0) for rows in (ra, rb, rc)]


def heavy_rows(block):
    row = lax.broadcasted_iota(jnp.int32, block.shape, 0)
    heavy = jnp.where(row == 6, block, block * block[6:7])
    return jnp.concatenate(pieces(heavy), 0).astype(BF16)


def force_kernel(stars_ref, state_ref, out_ref, met_ref, act_ref, sum_ref, feat_ref, prod_ref, weight_ref, col_ref):
    n_tiles = stars_ref.shape[0]
    n_blocks = N_YLO * N_CORE
    n_team = state_ref.shape[0] // n_blocks
    n_act = n_blocks * LANES
    sides = range(0, n_act, SIDE)

    for b in range(n_blocks):
        state = state_ref[b]
        for t in range(1, n_team):
            state = state + state_ref[t * n_blocks + b]
        xi, vi = predict(state[0:3], state[3:6], state[6:9], state[9:12], state[12:13])
        pack = jnp.concatenate([xi, vi, jnp.zeros((2, LANES), F32)], 0)
        at = b * LANES
        act_ref[:, at : at + LANES] = pack
        for k, rows in enumerate(active_rows(pack)):
            met_ref[:, k * n_act + at : k * n_act + at + LANES] = rows.astype(BF16)

    def block_of(t):
        line = stars_ref[t]
        members = line.shape[1] // 7
        rows = [line[:, q * members : (q + 1) * members] for q in range(7)]
        return jnp.concatenate(rows + [jnp.zeros((1, members), F32)], 0)

    def on_matrix(tile, side):
        return side < n_act // 2 or tile % CYCLE != CYCLE - 1

    def prepare(t, tile):
        cols = star_rows(block_of(t)).T
        feat_ref[...] = cols.astype(BF16)
        if not on_matrix(tile, n_act - 1):
            col_ref[...] = cols

    def products(side, tile):
        for k in (0, 1, 2) if on_matrix(tile, side) else (2,):
            at = k * n_act + side
            prod_ref[:, at : at + SIDE] = jnp.dot(
                feat_ref[...], met_ref[:, at : at + SIDE], preferred_element_type=F32
            )

    def weights(side, tile):
        cross = prod_ref[:, 2 * n_act + side : 2 * n_act + side + SIDE]
        if on_matrix(tile, side):
            r2 = prod_ref[:, side : side + SIDE] + prod_ref[:, n_act + side : n_act + side + SIDE]
        else:
            cols = col_ref[...]
            d = [cols[:, 123 + q : 124 + q] - act_ref[q : q + 1, side : side + SIDE] for q in range(3)]
            r2 = d[0] * d[0] + d[1] * d[1] + d[2] * d[2] + SOFTEN2
        inv = lax.rsqrt(r2)
        inv2 = inv * inv
        w = inv * inv2
        u = w * inv2 * cross
        for k, value in enumerate((w, u)):
            upper = value.astype(BF16)
            at = 2 * k * n_act + side
            weight_ref[:, at : at + SIDE] = upper
            at = at + n_act
            weight_ref[:, at : at + SIDE] = (value - upper.astype(F32)).astype(BF16)

    def add_up(heavy, side):
        for k in range(2):
            at = 2 * k * n_act + side
            upper, lower = weight_ref[:, at : at + SIDE], weight_ref[:, at + n_act : at + n_act + SIDE]
            part = jnp.dot(heavy, upper, preferred_element_type=F32) + jnp.dot(
                heavy, lower, preferred_element_type=F32
            )
            at = k * n_act + side
            sum_ref[:, at : at + SIDE] = sum_ref[:, at : at + SIDE] + part

    sum_ref[...] = jnp.zeros_like(sum_ref)
    prepare(0, 0)
    for side in sides:
        products(side, 0)
    prepare(1, 1)

    def one_cycle(c, _):
        for tile in range(CYCLE):
            t = c * CYCLE + tile
            heavy = heavy_rows(block_of(t))
            for side in sides:
                weights(side, tile)
                products(side, tile + 1)
                add_up(heavy, side)
            prepare(jnp.minimum(t + 2, n_tiles - 1), tile + 2)
        return 0

    lax.fori_loop(0, n_tiles // CYCLE, one_cycle, 0, unroll=2)
    sums = sum_ref[16:24, :] + sum_ref[8:16, :] + sum_ref[0:8, :]
    sw, su = sums[:, :n_act], sums[:, n_act:]
    xi, vi = act_ref[0:3, :], act_ref[3:6, :]
    a = sw[0:3] - xi * sw[6:7]
    j = (sw[3:6] - vi * sw[6:7]) - 3.0 * (su[0:3] - xi * su[6:7])
    part = jnp.concatenate([a, j, jnp.zeros((2, n_act), F32)], 0)
    for b in range(n_blocks):
        for t in range(n_team):
            out_ref[t * n_blocks + b] = part[:, b * LANES : (b + 1) * LANES]


def correct_kernel(part_ref, state_ref, phase_ref, force_ref, higher_ref):
    n = part_ref.shape[0]
    n_blocks = N_YLO * N_CORE
    mine = lax.axis_index("y") * N_CORE + lax.axis_index("core")
    total = part_ref[0]
    for k in range(1, n):
        total = total + part_ref[k]
    own = state_ref[mine]
    for t in range(1, n // n_blocks):
        own = own + state_ref[t * n_blocks + mine]
    x0, v0, a0, j0, dt = (own[0:3], own[3:6], own[6:9], own[9:12], own[12:13])
    a1, j1 = (total[0:3], total[3:6])
    v1 = v0 + (a0 + a1) * dt / 2.0 + (j0 - j1) * dt * dt / 12.0
    x1 = x0 + (v0 + v1) * dt / 2.0 + (a0 - a1) * dt * dt / 12.0
    snap = -6.0 * (a0 - a1) - dt * (4.0 * j0 + 2.0 * j1)
    crackle = 12.0 * (a0 - a1) + 6.0 * dt * (j0 + j1)
    phase_ref[...] = jnp.concatenate([x1, v1], 0)
    force_ref[...] = total[0:6]
    higher_ref[...] = jnp.concatenate([snap, crackle], 0)


def shards(sizes, position, velocity, old_accel, old_jerk, mass, elapsed, active_slot, active_owner):
    members = position.shape[1]
    actives = active_slot.shape[0]
    n_gather = sizes["x"] * sizes["z"]
    n_reduce = sizes["team"] * sizes["y"] * sizes["core"]
    n_blocks = sizes["y"] * sizes["core"]
    elapsed = elapsed.reshape(1, members)
    state = pl.pallas_call(
        state_kernel, out_shape=jax.ShapeDtypeStruct((n_reduce, 16, actives), F32), name="state"
    )(
        position, velocity, old_accel, old_jerk, elapsed,
        active_slot.reshape(1, actives), active_owner.reshape(1, actives),
    )
    stars = pl.pallas_call(
        star_kernel,
        out_shape=jax.ShapeDtypeStruct((n_gather, 1, 7 * members), F32),
        compiler_params=pltpu.CompilerParams(vmem_limit_bytes=SMALL),
        name="stars",
    )(position, velocity, old_accel, old_jerk, mass.reshape(1, members), elapsed)
    state = lax.all_to_all(state, REDUCE, 0, 0, tiled=True)
    stars = lax.all_to_all(stars, GATHER, 0, 0, tiled=True)
    n_act = n_blocks * actives
    part = pl.pallas_call(
        force_kernel,
        out_shape=jax.ShapeDtypeStruct((n_reduce, 8, actives), F32),
        scratch_shapes=[
            pltpu.VMEM((LANES, 3 * n_act), BF16),
            pltpu.VMEM((8, n_act), F32),
            pltpu.VMEM((24, 2 * n_act), F32),
            pltpu.VMEM((members, LANES), BF16),
            pltpu.VMEM((members, 3 * n_act), F32),
            pltpu.VMEM((members, 4 * n_act), BF16),
            pltpu.VMEM((members, LANES), F32),
        ],
        compiler_params=pltpu.CompilerParams(vmem_limit_bytes=16 * 1024 * 1024),
        name="force",
    )(stars, state)
    part = lax.all_to_all(part, REDUCE, 0, 0, tiled=True)
    out = jax.ShapeDtypeStruct((6, actives), F32)
    return pl.pallas_call(
        correct_kernel,
        out_shape=(out, out, out),
        compiler_params=pltpu.CompilerParams(vmem_limit_bytes=SMALL),
        name="correct",
    )(part, state)


def solution(mesh):
    n_team = mesh.shape["team"]
    fine = Mesh(
        mesh.devices.reshape(n_team, N_X, N_YLO, N_Z, N_CORE), ("team", "x", "y", "z", "core")
    )
    blk = ("x", "y", "z", "core")
    whole = ("team",) + blk
    placed = (
        P(None, whole), P(None, whole), P(None, whole), P(None, whole),
        P(whole), P(whole), P(blk), P(blk),
    )
    return jax.shard_map(
        functools.partial(shards, dict(fine.shape)),
        mesh=fine,
        in_specs=placed,
        out_specs=(P(None, blk), P(None, blk), P(None, blk)),
        check_vma=False,
    )
```

```python
import functools
import jax
import jax.numpy as jnp
from jax import lax
from jax.experimental import pallas as pl
from jax.experimental.pallas import tpu as pltpu
from jax.sharding import Mesh, PartitionSpec as P

SOFTEN2 = 0.0001
N_X, N_YLO, N_Z, N_CORE = 4, 2, 8, 2
LANES = 128
GATHER = ("x", "z")
REDUCE = ("team", "y", "core")
SIDE = 256
CYCLE = 4
SMALL = 4 * 1024 * 1024
N_STATE = 13
N_FORCE = 6
F32 = jnp.float32
BF16 = jnp.bfloat16


def predict(x, v, a, j, h):
    xp = x + h * (v + h * (a / 2.0 + h * j / 6.0))
    vp = v + h * (a + h * j / 2.0)
    return (xp, vp)


def in_line(value, count):
    return jnp.concatenate([value[q : q + 1] for q in range(count)], axis=1)


def in_rows(line, count):
    width = line.shape[1] // count
    return jnp.concatenate([line[:, q * width : (q + 1) * width] for q in range(count)], axis=0)


def state_kernel(x_ref, v_ref, a_ref, j_ref, h_ref, slot_ref, owner_ref, state_ref):
    members, actives = x_ref.shape[1], slot_ref.shape[1]
    team = lax.axis_index("team")
    wanted = jnp.where(owner_ref[...] == team, slot_ref[...], -1)
    chooser = (lax.broadcasted_iota(jnp.int32, (members, actives), 0) == wanted).astype(F32)
    state = jnp.concatenate(
        [x_ref[...], v_ref[...], a_ref[...], j_ref[...], h_ref[...], jnp.zeros((3, members), F32)], axis=0
    )
    chosen = jnp.dot(state, chooser, precision=lax.Precision.HIGHEST, preferred_element_type=F32)
    line = in_line(chosen, N_STATE)
    for k in range(state_ref.shape[0]):
        state_ref[k] = line


def star_kernel(x_ref, v_ref, a_ref, j_ref, m_ref, h_ref, stars_ref):
    xp, vp = predict(x_ref[...], v_ref[...], a_ref[...], j_ref[...], h_ref[...])
    rows = [value[q : q + 1] for value in (xp, vp) for q in range(3)] + [m_ref[...]]
    star = jnp.concatenate(rows, axis=1)
    for k in range(stars_ref.shape[0]):
        stars_ref[k] = star


def rounded(value):
    return value.astype(BF16).astype(F32)


def pieces(value):
    first = rounded(value)
    rest = value - first
    second = rounded(rest)
    return [first, second, rest - second]


def grid_pieces(value):
    high = jnp.round(value * 128.0) * (1.0 / 128.0)
    first = rounded(high)
    low = value - high
    third = rounded(low)
    return high, low, [first, high - first, third, low - third]


def star_rows(block):
    row = lax.broadcasted_iota(jnp.int32, block.shape, 0)

    def roll(value, shift):
        return pltpu.roll(value, shift, 0)

    moving = jnp.where(row < 6, block, 0.0)
    high, low, p = grid_pieces(moving)
    square = high * high
    twice = low * (2.0 * high + low)
    coarse = roll(square, 6) + roll(square, 5) + roll(square, 4)
    fine = roll(twice, 7) + roll(twice, 6) + roll(twice, 5)
    own = pieces(jnp.where(row == 6, coarse, jnp.where(row == 7, fine, 0.0)))
    both = moving * roll(moving, 5)
    cross = both + roll(both, 7) + roll(both, 6)
    c = pieces(jnp.broadcast_to(cross[0:1], cross.shape))
    last = jnp.where(row < 6, roll(block, 3), 0.0)
    for k in range(3):
        last = jnp.where(row == k, c[k], last)
    stack = []
    for k in range(3):
        stack += [p[k] + own[k]] * 4
    stack += [jnp.where(row == 6, 1.0, p[3])] * 3 + [last]
    return jnp.concatenate(stack, 0)


def sum3(rows):
    return rows[0:1] + rows[1:2] + rows[2:3]


def active_rows(pack):
    n = pack.shape[1]
    high, low, p = grid_pieces(pack)
    coarse = pieces(sum3(high[0:3] * high[0:3]))
    fine = pieces(sum3(low[0:3] * (2.0 * high[0:3] + low[0:3])) + SOFTEN2)
    cross = pieces(sum3(pack[0:3] * pack[3:6]))
    zero3, zero, one = jnp.zeros((3, n), F32), jnp.zeros((1, n), F32), jnp.ones((1, n), F32)
    ra, rb, rc = [], [], []
    for k in range(4):
        for l in range(4 if k < 3 else 3):
            is_coarse = k < 2 and l < 2
            unit = one if (l == 0 and k < 3) else zero
            twice = -2.0 * p[l][0:3]
            last = k == 3
            ra.append(jnp.concatenate([twice if is_coarse else zero3, zero3, coarse[l] if last else unit, zero], 0))
            rb.append(jnp.concatenate([zero3 if is_coarse else twice, zero3, fine[l] if last else zero, unit], 0))
            rc.append(jnp.concatenate([-p[l][3:6], -p[l][0:3], cross[l] if last else zero, zero], 0))
    ra.append(jnp.zeros((8, n), F32))
    rb.append(jnp.zeros((8, n), F32))
    rc.append(jnp.concatenate([jnp.ones((3, n), F32), jnp.zeros((5, n), F32)], 0))
    return [jnp.concatenate(rows, 0) for rows in (ra, rb, rc)]


def heavy_rows(block):
    row = lax.broadcasted_iota(jnp.int32, block.shape, 0)
    heavy = jnp.where(row == 6, block, block * block[6:7])
    return jnp.concatenate(pieces(heavy), 0).astype(BF16)


def force_kernel(stars_ref, state_ref, out_ref, met_ref, act_ref, sum_ref, feat_ref, prod_ref, weight_ref, col_ref):
    n_tiles = stars_ref.shape[0]
    n_blocks = N_YLO * N_CORE
    n_team = state_ref.shape[0] // n_blocks
    n_act = n_blocks * LANES
    sides = range(0, n_act, SIDE)

    for b in range(n_blocks):
        state = state_ref[b]
        for t in range(1, n_team):
            state = state + state_ref[t * n_blocks + b]
        state = in_rows(state, N_STATE)
        xi, vi = predict(state[0:3], state[3:6], state[6:9], state[9:12], state[12:13])
        pack = jnp.concatenate([xi, vi, jnp.zeros((2, LANES), F32)], 0)
        at = b * LANES
        act_ref[:, at : at + LANES] = pack
        for k, rows in enumerate(active_rows(pack)):
            met_ref[:, k * n_act + at : k * n_act + at + LANES] = rows.astype(BF16)

    def block_of(t):
        line = stars_ref[t]
        members = line.shape[1] // 7
        rows = [line[:, q * members : (q + 1) * members] for q in range(7)]
        return jnp.concatenate(rows + [jnp.zeros((1, members), F32)], 0)

    def on_matrix(tile, side):
        return side < n_act // 2 or tile % CYCLE != CYCLE - 1

    def prepare(t, tile):
        cols = star_rows(block_of(t)).T
        feat_ref[...] = cols.astype(BF16)
        if not on_matrix(tile, n_act - 1):
            col_ref[...] = cols

    def products(side, tile):
        for k in (0, 1, 2) if on_matrix(tile, side) else (2,):
            at = k * n_act + side
            prod_ref[:, at : at + SIDE] = jnp.dot(
                feat_ref[...], met_ref[:, at : at + SIDE], preferred_element_type=F32
            )

    def weights(side, tile):
        cross = prod_ref[:, 2 * n_act + side : 2 * n_act + side + SIDE]
        if on_matrix(tile, side):
            r2 = prod_ref[:, side : side + SIDE] + prod_ref[:, n_act + side : n_act + side + SIDE]
        else:
            cols = col_ref[...]
            d = [cols[:, 123 + q : 124 + q] - act_ref[q : q + 1, side : side + SIDE] for q in range(3)]
            r2 = d[0] * d[0] + d[1] * d[1] + d[2] * d[2] + SOFTEN2
        inv = lax.rsqrt(r2)
        inv2 = inv * inv
        w = inv * inv2
        u = w * inv2 * cross
        for k, value in enumerate((w, u)):
            upper = value.astype(BF16)
            at = 2 * k * n_act + side
            weight_ref[:, at : at + SIDE] = upper
            at = at + n_act
            weight_ref[:, at : at + SIDE] = (value - upper.astype(F32)).astype(BF16)

    def add_up(heavy, side):
        for k in range(2):
            at = 2 * k * n_act + side
            upper, lower = weight_ref[:, at : at + SIDE], weight_ref[:, at + n_act : at + n_act + SIDE]
            part = jnp.dot(heavy, upper, preferred_element_type=F32) + jnp.dot(
                heavy, lower, preferred_element_type=F32
            )
            at = k * n_act + side
            sum_ref[:, at : at + SIDE] = sum_ref[:, at : at + SIDE] + part

    sum_ref[...] = jnp.zeros_like(sum_ref)
    prepare(0, 0)
    for side in sides:
        products(side, 0)
    prepare(1, 1)

    def one_cycle(c, _):
        for tile in range(CYCLE):
            t = c * CYCLE + tile
            heavy = heavy_rows(block_of(t))
            for side in sides:
                weights(side, tile)
                products(side, tile + 1)
                add_up(heavy, side)
            prepare(jnp.minimum(t + 2, n_tiles - 1), tile + 2)
        return 0

    lax.fori_loop(0, n_tiles // CYCLE, one_cycle, 0, unroll=2)
    sums = sum_ref[16:24, :] + sum_ref[8:16, :] + sum_ref[0:8, :]
    sw, su = sums[:, :n_act], sums[:, n_act:]
    xi, vi = act_ref[0:3, :], act_ref[3:6, :]
    a = sw[0:3] - xi * sw[6:7]
    j = (sw[3:6] - vi * sw[6:7]) - 3.0 * (su[0:3] - xi * su[6:7])
    part = jnp.concatenate([a, j], 0)
    for b in range(n_blocks):
        line = in_line(part[:, b * LANES : (b + 1) * LANES], N_FORCE)
        for t in range(n_team):
            out_ref[t * n_blocks + b] = line


def correct_kernel(part_ref, state_ref, phase_ref, force_ref, higher_ref):
    n = part_ref.shape[0]
    n_blocks = N_YLO * N_CORE
    mine = lax.axis_index("y") * N_CORE + lax.axis_index("core")
    total = part_ref[0]
    for k in range(1, n):
        total = total + part_ref[k]
    own = state_ref[mine]
    for t in range(1, n // n_blocks):
        own = own + state_ref[t * n_blocks + mine]
    own, total = in_rows(own, N_STATE), in_rows(total, N_FORCE)
    x0, v0, a0, j0, dt = (own[0:3], own[3:6], own[6:9], own[9:12], own[12:13])
    a1, j1 = (total[0:3], total[3:6])
    v1 = v0 + (a0 + a1) * dt / 2.0 + (j0 - j1) * dt * dt / 12.0
    x1 = x0 + (v0 + v1) * dt / 2.0 + (a0 - a1) * dt * dt / 12.0
    snap = -6.0 * (a0 - a1) - dt * (4.0 * j0 + 2.0 * j1)
    crackle = 12.0 * (a0 - a1) + 6.0 * dt * (j0 + j1)
    phase_ref[...] = jnp.concatenate([x1, v1], 0)
    force_ref[...] = total[0:6]
    higher_ref[...] = jnp.concatenate([snap, crackle], 0)


def shards(sizes, position, velocity, old_accel, old_jerk, mass, elapsed, active_slot, active_owner):
    members = position.shape[1]
    actives = active_slot.shape[0]
    n_gather = sizes["x"] * sizes["z"]
    n_reduce = sizes["team"] * sizes["y"] * sizes["core"]
    n_blocks = sizes["y"] * sizes["core"]
    elapsed = elapsed.reshape(1, members)
    state = pl.pallas_call(
        state_kernel,
        out_shape=jax.ShapeDtypeStruct((n_reduce, 1, N_STATE * actives), F32),
        compiler_params=pltpu.CompilerParams(vmem_limit_bytes=SMALL),
        name="state",
    )(
        position, velocity, old_accel, old_jerk, elapsed,
        active_slot.reshape(1, actives), active_owner.reshape(1, actives),
    )
    stars = pl.pallas_call(
        star_kernel,
        out_shape=jax.ShapeDtypeStruct((n_gather, 1, 7 * members), F32),
        name="stars",
    )(position, velocity, old_accel, old_jerk, mass.reshape(1, members), elapsed)
    stars = lax.all_to_all(stars, GATHER, 0, 0, tiled=True)
    state, stars = lax.optimization_barrier((state, stars))
    state = lax.all_to_all(state, REDUCE, 0, 0, tiled=True)
    n_act = n_blocks * actives
    part = pl.pallas_call(
        force_kernel,
        out_shape=jax.ShapeDtypeStruct((n_reduce, 1, N_FORCE * actives), F32),
        scratch_shapes=[
            pltpu.VMEM((LANES, 3 * n_act), BF16),
            pltpu.VMEM((8, n_act), F32),
            pltpu.VMEM((24, 2 * n_act), F32),
            pltpu.VMEM((members, LANES), BF16),
            pltpu.VMEM((members, 3 * n_act), F32),
            pltpu.VMEM((members, 4 * n_act), BF16),
            pltpu.VMEM((members, LANES), F32),
        ],
        compiler_params=pltpu.CompilerParams(vmem_limit_bytes=16 * 1024 * 1024),
        name="force",
    )(stars, state)
    part = lax.all_to_all(part, REDUCE, 0, 0, tiled=True)
    out = jax.ShapeDtypeStruct((6, actives), F32)
    return pl.pallas_call(
        correct_kernel,
        out_shape=(out, out, out),
        compiler_params=pltpu.CompilerParams(vmem_limit_bytes=SMALL),
        name="correct",
    )(part, state)


def solution(mesh):
    n_team = mesh.shape["team"]
    fine = Mesh(
        mesh.devices.reshape(n_team, N_X, N_YLO, N_Z, N_CORE), ("team", "x", "y", "z", "core")
    )
    blk = ("x", "y", "z", "core")
    whole = ("team",) + blk
    placed = (
        P(None, whole), P(None, whole), P(None, whole), P(None, whole),
        P(whole), P(whole), P(blk), P(blk),
    )
    return jax.shard_map(
        functools.partial(shards, dict(fine.shape)),
        mesh=fine,
        in_specs=placed,
        out_specs=(P(None, blk), P(None, blk), P(None, blk)),
        check_vma=False,
    )
```

```python
import functools
import jax
import jax.numpy as jnp
from jax import lax
from jax.experimental import pallas as pl
from jax.experimental.pallas import tpu as pltpu
from jax.sharding import Mesh, PartitionSpec as P

SOFTEN2 = 0.0001
N_X, N_YLO, N_Z, N_CORE = 4, 2, 8, 2
LANES = 128
GATHER = ("x", "z")
REDUCE = ("team", "y", "core")
SIDE = 256
CYCLE = 4
SMALL = 4 * 1024 * 1024
N_STATE = 13
N_FORCE = 6
F32 = jnp.float32
BF16 = jnp.bfloat16


def predict(x, v, a, j, h):
    xp = x + h * (v + h * (a / 2.0 + h * j / 6.0))
    vp = v + h * (a + h * j / 2.0)
    return (xp, vp)


def in_line(value, count):
    return jnp.concatenate([value[q : q + 1] for q in range(count)], axis=1)


def in_rows(line, count):
    width = line.shape[1] // count
    return jnp.concatenate([line[:, q * width : (q + 1) * width] for q in range(count)], axis=0)


def state_kernel(x_ref, v_ref, a_ref, j_ref, h_ref, slot_ref, owner_ref, state_ref):
    members, actives = x_ref.shape[1], slot_ref.shape[1]
    team = lax.axis_index("team")
    wanted = jnp.where(owner_ref[...] == team, slot_ref[...], -1)
    chooser = (lax.broadcasted_iota(jnp.int32, (members, actives), 0) == wanted).astype(F32)
    state = jnp.concatenate(
        [x_ref[...], v_ref[...], a_ref[...], j_ref[...], h_ref[...], jnp.zeros((3, members), F32)], axis=0
    )
    chosen = jnp.dot(state, chooser, precision=lax.Precision.HIGHEST, preferred_element_type=F32)
    line = in_line(chosen, N_STATE)
    for k in range(state_ref.shape[0]):
        state_ref[k] = line


def star_kernel(x_ref, v_ref, a_ref, j_ref, m_ref, h_ref, stars_ref):
    xp, vp = predict(x_ref[...], v_ref[...], a_ref[...], j_ref[...], h_ref[...])
    rows = [value[q : q + 1] for value in (xp, vp) for q in range(3)] + [m_ref[...]]
    star = jnp.concatenate(rows, axis=1)
    for k in range(stars_ref.shape[0]):
        stars_ref[k] = star


def rounded(value):
    return value.astype(BF16).astype(F32)


def pieces(value):
    first = rounded(value)
    rest = value - first
    second = rounded(rest)
    return [first, second, rest - second]


def grid_pieces(value):
    high = jnp.round(value * 128.0) * (1.0 / 128.0)
    first = rounded(high)
    low = value - high
    third = rounded(low)
    return high, low, [first, high - first, third, low - third]


def star_rows(block):
    row = lax.broadcasted_iota(jnp.int32, block.shape, 0)

    def roll(value, shift):
        return pltpu.roll(value, shift, 0)

    moving = jnp.where(row < 6, block, 0.0)
    high, low, p = grid_pieces(moving)
    square = high * high
    twice = low * (2.0 * high + low)
    coarse = roll(square, 6) + roll(square, 5) + roll(square, 4)
    fine = roll(twice, 7) + roll(twice, 6) + roll(twice, 5)
    own = pieces(jnp.where(row == 6, coarse, jnp.where(row == 7, fine, 0.0)))
    both = moving * roll(moving, 5)
    cross = both + roll(both, 7) + roll(both, 6)
    c = pieces(jnp.broadcast_to(cross[0:1], cross.shape))
    last = jnp.where(row < 6, roll(block, 3), 0.0)
    for k in range(3):
        last = jnp.where(row == k, c[k], last)
    stack = []
    for k in range(3):
        stack += [p[k] + own[k]] * 4
    stack += [jnp.where(row == 6, 1.0, p[3])] * 3 + [last]
    return jnp.concatenate(stack, 0)


def sum3(rows):
    return rows[0:1] + rows[1:2] + rows[2:3]


def active_rows(pack):
    n = pack.shape[1]
    high, low, p = grid_pieces(pack)
    coarse = pieces(sum3(high[0:3] * high[0:3]))
    fine = pieces(sum3(low[0:3] * (2.0 * high[0:3] + low[0:3])) + SOFTEN2)
    cross = pieces(sum3(pack[0:3] * pack[3:6]))
    zero3, zero, one = jnp.zeros((3, n), F32), jnp.zeros((1, n), F32), jnp.ones((1, n), F32)
    ra, rb, rc = [], [], []
    for k in range(4):
        for l in range(4 if k < 3 else 3):
            is_coarse = k < 2 and l < 2
            unit = one if (l == 0 and k < 3) else zero
            twice = -2.0 * p[l][0:3]
            last = k == 3
            ra.append(jnp.concatenate([twice if is_coarse else zero3, zero3, coarse[l] if last else unit, zero], 0))
            rb.append(jnp.concatenate([zero3 if is_coarse else twice, zero3, fine[l] if last else zero, unit], 0))
            rc.append(jnp.concatenate([-p[l][3:6], -p[l][0:3], cross[l] if last else zero, zero], 0))
    ra.append(jnp.zeros((8, n), F32))
    rb.append(jnp.zeros((8, n), F32))
    rc.append(jnp.concatenate([jnp.ones((3, n), F32), jnp.zeros((5, n), F32)], 0))
    return [jnp.concatenate(rows, 0) for rows in (ra, rb, rc)]


def heavy_rows(block):
    row = lax.broadcasted_iota(jnp.int32, block.shape, 0)
    heavy = jnp.where(row == 6, block, block * block[6:7])
    return jnp.concatenate(pieces(heavy), 0).astype(BF16)


def force_kernel(
    stars_ref, state_ref, slot_ref, owner_ref, out_ref, met_ref, act_ref, mid_ref, sum_ref, feat_ref, prod_ref, weight_ref, col_ref
):
    n_tiles = stars_ref.shape[0]
    n_blocks = N_YLO * N_CORE
    n_team = state_ref.shape[0] // n_blocks
    n_act = n_blocks * LANES
    sides = range(0, n_act, SIDE)

    for b in range(n_blocks):
        state = state_ref[b]
        for t in range(1, n_team):
            state = state + state_ref[t * n_blocks + b]
        state = in_rows(state, N_STATE)
        xi, vi = predict(state[0:3], state[3:6], state[6:9], state[9:12], state[12:13])
        pack = jnp.concatenate([xi, vi, jnp.zeros((2, LANES), F32)], 0)
        act_ref[:, b * LANES : (b + 1) * LANES] = pack

    mean = jnp.sum(act_ref[...], axis=1, keepdims=True) * (1.0 / n_act)
    mid_ref[...] = jnp.broadcast_to(jnp.round(mean * 2.0) * 0.5, mid_ref.shape)
    for b in range(n_blocks):
        at = b * LANES
        pack = act_ref[:, at : at + LANES] - mid_ref[:, :LANES]
        act_ref[:, at : at + LANES] = pack
        for k, rows in enumerate(active_rows(pack)):
            met_ref[:, k * n_act + at : k * n_act + at + LANES] = rows.astype(BF16)

    def block_of(t):
        line = stars_ref[t]
        members = line.shape[1] // 7
        rows = [line[:, q * members : (q + 1) * members] for q in range(7)]
        return jnp.concatenate(rows + [jnp.zeros((1, members), F32)], 0) - mid_ref[...]

    def on_matrix(tile, side):
        return side < n_act // 2 or tile % CYCLE != CYCLE - 1

    def prepare(t, tile):
        cols = star_rows(block_of(t)).T
        feat_ref[...] = cols.astype(BF16)
        if not on_matrix(tile, n_act - 1):
            col_ref[...] = cols

    def products(side, tile):
        for k in (0, 1, 2) if on_matrix(tile, side) else (2,):
            at = k * n_act + side
            prod_ref[:, at : at + SIDE] = jnp.dot(
                feat_ref[...], met_ref[:, at : at + SIDE], preferred_element_type=F32
            )

    def weights(side, tile, same=None):
        cross = prod_ref[:, 2 * n_act + side : 2 * n_act + side + SIDE]
        if on_matrix(tile, side):
            r2 = prod_ref[:, side : side + SIDE] + prod_ref[:, n_act + side : n_act + side + SIDE]
        else:
            cols = col_ref[...]
            d = [cols[:, 123 + q : 124 + q] - act_ref[q : q + 1, side : side + SIDE] for q in range(3)]
            r2 = d[0] * d[0] + d[1] * d[1] + d[2] * d[2] + SOFTEN2
        inv = lax.rsqrt(r2)
        inv2 = inv * inv
        w = inv * inv2
        u = w * inv2 * cross
        if same is not None:
            w, u = (jnp.where(same[:, side : side + SIDE], 0.0, value) for value in (w, u))
        for k, value in enumerate((w, u)):
            upper = value.astype(BF16)
            at = 2 * k * n_act + side
            weight_ref[:, at : at + SIDE] = upper
            at = at + n_act
            weight_ref[:, at : at + SIDE] = (value - upper.astype(F32)).astype(BF16)

    def add_up(heavy, side):
        for k in range(2):
            at = 2 * k * n_act + side
            upper, lower = weight_ref[:, at : at + SIDE], weight_ref[:, at + n_act : at + n_act + SIDE]
            part = jnp.dot(heavy, upper, preferred_element_type=F32) + jnp.dot(
                heavy, lower, preferred_element_type=F32
            )
            at = k * n_act + side
            sum_ref[:, at : at + SIDE] = sum_ref[:, at : at + SIDE] + part

    here = lax.axis_index("x") * N_Z + lax.axis_index("z")
    mine = lax.axis_index("y") * N_CORE + lax.axis_index("core")
    wanted = jnp.where(owner_ref[...] == lax.axis_index("team"), slot_ref[...], -1)
    wanted = jnp.concatenate([jnp.where(mine == b, wanted, -1) for b in range(n_blocks)], 1)
    sum_ref[...] = jnp.zeros_like(sum_ref)
    prepare(here, 0)
    for side in sides:
        products(side, 0)
    same = lax.broadcasted_iota(jnp.int32, (feat_ref.shape[0], n_act), 0) == wanted
    heavy = heavy_rows(block_of(here))
    for side in sides:
        weights(side, 0, same)
        add_up(heavy, side)
    prepare(0, 0)
    for side in sides:
        products(side, 0)
    prepare(1, 1)

    def one_cycle(c, _):
        for tile in range(CYCLE):
            t = c * CYCLE + tile
            heavy = heavy_rows(block_of(t)) * (t != here).astype(BF16)
            for side in sides:
                weights(side, tile)
                products(side, tile + 1)
                add_up(heavy, side)
            prepare(jnp.minimum(t + 2, n_tiles - 1), tile + 2)
        return 0

    lax.fori_loop(0, n_tiles // CYCLE, one_cycle, 0, unroll=2)
    sums = sum_ref[16:24, :] + sum_ref[8:16, :] + sum_ref[0:8, :]
    sw, su = sums[:, :n_act], sums[:, n_act:]
    xi, vi = act_ref[0:3, :], act_ref[3:6, :]
    a = sw[0:3] - xi * sw[6:7]
    j = (sw[3:6] - vi * sw[6:7]) - 3.0 * (su[0:3] - xi * su[6:7])
    part = jnp.concatenate([a, j], 0)
    for b in range(n_blocks):
        line = in_line(part[:, b * LANES : (b + 1) * LANES], N_FORCE)
        for t in range(n_team):
            out_ref[t * n_blocks + b] = line


def correct_kernel(part_ref, state_ref, phase_ref, force_ref, higher_ref):
    n = part_ref.shape[0]
    n_blocks = N_YLO * N_CORE
    mine = lax.axis_index("y") * N_CORE + lax.axis_index("core")
    total = part_ref[0]
    for k in range(1, n):
        total = total + part_ref[k]
    own = state_ref[mine]
    for t in range(1, n // n_blocks):
        own = own + state_ref[t * n_blocks + mine]
    own, total = in_rows(own, N_STATE), in_rows(total, N_FORCE)
    x0, v0, a0, j0, dt = (own[0:3], own[3:6], own[6:9], own[9:12], own[12:13])
    a1, j1 = (total[0:3], total[3:6])
    v1 = v0 + (a0 + a1) * dt / 2.0 + (j0 - j1) * dt * dt / 12.0
    x1 = x0 + (v0 + v1) * dt / 2.0 + (a0 - a1) * dt * dt / 12.0
    snap = -6.0 * (a0 - a1) - dt * (4.0 * j0 + 2.0 * j1)
    crackle = 12.0 * (a0 - a1) + 6.0 * dt * (j0 + j1)
    phase_ref[...] = jnp.concatenate([x1, v1], 0)
    force_ref[...] = total[0:6]
    higher_ref[...] = jnp.concatenate([snap, crackle], 0)


def shards(sizes, position, velocity, old_accel, old_jerk, mass, elapsed, active_slot, active_owner):
    members = position.shape[1]
    actives = active_slot.shape[0]
    n_gather = sizes["x"] * sizes["z"]
    n_reduce = sizes["team"] * sizes["y"] * sizes["core"]
    n_blocks = sizes["y"] * sizes["core"]
    elapsed = elapsed.reshape(1, members)
    state = pl.pallas_call(
        state_kernel,
        out_shape=jax.ShapeDtypeStruct((n_reduce, 1, N_STATE * actives), F32),
        compiler_params=pltpu.CompilerParams(vmem_limit_bytes=SMALL),
        name="state",
    )(
        position, velocity, old_accel, old_jerk, elapsed,
        active_slot.reshape(1, actives), active_owner.reshape(1, actives),
    )
    stars = pl.pallas_call(
        star_kernel,
        out_shape=jax.ShapeDtypeStruct((n_gather, 1, 7 * members), F32),
        name="stars",
    )(position, velocity, old_accel, old_jerk, mass.reshape(1, members), elapsed)
    stars = lax.all_to_all(stars, GATHER, 0, 0, tiled=True)
    state, stars = lax.optimization_barrier((state, stars))
    state = lax.all_to_all(state, REDUCE, 0, 0, tiled=True)
    n_act = n_blocks * actives
    part = pl.pallas_call(
        force_kernel,
        out_shape=jax.ShapeDtypeStruct((n_reduce, 1, N_FORCE * actives), F32),
        scratch_shapes=[
            pltpu.VMEM((LANES, 3 * n_act), BF16),
            pltpu.VMEM((8, n_act), F32),
            pltpu.VMEM((8, members), F32),
            pltpu.VMEM((24, 2 * n_act), F32),
            pltpu.VMEM((members, LANES), BF16),
            pltpu.VMEM((members, 3 * n_act), F32),
            pltpu.VMEM((members, 4 * n_act), BF16),
            pltpu.VMEM((members, LANES), F32),
        ],
        compiler_params=pltpu.CompilerParams(vmem_limit_bytes=16 * 1024 * 1024),
        name="force",
    )(stars, state, active_slot.reshape(1, actives), active_owner.reshape(1, actives))
    part = lax.all_to_all(part, REDUCE, 0, 0, tiled=True)
    out = jax.ShapeDtypeStruct((6, actives), F32)
    return pl.pallas_call(
        correct_kernel,
        out_shape=(out, out, out),
        compiler_params=pltpu.CompilerParams(vmem_limit_bytes=SMALL),
        name="correct",
    )(part, state)


def solution(mesh):
    n_team = mesh.shape["team"]
    fine = Mesh(
        mesh.devices.reshape(n_team, N_X, N_YLO, N_Z, N_CORE), ("team", "x", "y", "z", "core")
    )
    blk = ("x", "y", "z", "core")
    whole = ("team",) + blk
    placed = (
        P(None, whole), P(None, whole), P(None, whole), P(None, whole),
        P(whole), P(whole), P(blk), P(blk),
    )
    return jax.shard_map(
        functools.partial(shards, dict(fine.shape)),
        mesh=fine,
        in_specs=placed,
        out_specs=(P(None, blk), P(None, blk), P(None, blk)),
        check_vma=False,
    )
```

```python
import functools
import jax
import jax.numpy as jnp
from jax import lax
from jax.experimental import pallas as pl
from jax.experimental.pallas import tpu as pltpu
from jax.sharding import Mesh, PartitionSpec as P

SOFTEN2 = 0.0001
N_X, N_YLO, N_Z, N_CORE = 4, 2, 8, 2
LANES = 128
GATHER = ("x", "z")
REDUCE = ("team", "y", "core")
SIDE = 256
CYCLE = 4
SMALL = 4 * 1024 * 1024
N_STATE = 13
N_FORCE = 6
F32 = jnp.float32
BF16 = jnp.bfloat16


def predict(x, v, a, j, h):
    xp = x + h * (v + h * (a / 2.0 + h * j / 6.0))
    vp = v + h * (a + h * j / 2.0)
    return (xp, vp)


def in_line(value, count):
    return jnp.concatenate([value[q : q + 1] for q in range(count)], axis=1)


def in_rows(line, count):
    width = line.shape[1] // count
    return jnp.concatenate([line[:, q * width : (q + 1) * width] for q in range(count)], axis=0)


def state_kernel(x_ref, v_ref, a_ref, j_ref, h_ref, slot_ref, owner_ref, state_ref):
    members, actives = x_ref.shape[1], slot_ref.shape[1]
    team = lax.axis_index("team")
    wanted = jnp.where(owner_ref[...] == team, slot_ref[...], -1)
    chooser = (lax.broadcasted_iota(jnp.int32, (members, actives), 0) == wanted).astype(F32)
    state = jnp.concatenate(
        [x_ref[...], v_ref[...], a_ref[...], j_ref[...], h_ref[...], jnp.zeros((3, members), F32)], axis=0
    )
    chosen = jnp.dot(state, chooser, precision=lax.Precision.HIGHEST, preferred_element_type=F32)
    line = in_line(chosen, N_STATE)
    for k in range(state_ref.shape[0]):
        state_ref[k] = line


def star_kernel(x_ref, v_ref, a_ref, j_ref, m_ref, h_ref, stars_ref):
    xp, vp = predict(x_ref[...], v_ref[...], a_ref[...], j_ref[...], h_ref[...])
    rows = [value[q : q + 1] for value in (xp, vp) for q in range(3)] + [m_ref[...]]
    star = jnp.concatenate(rows, axis=1)
    for k in range(stars_ref.shape[0]):
        stars_ref[k] = star


def rounded(value):
    return value.astype(BF16).astype(F32)


def pieces(value):
    first = rounded(value)
    rest = value - first
    second = rounded(rest)
    return [first, second, rest - second]


def grid_pieces(value):
    high = jnp.round(value * 128.0) * (1.0 / 128.0)
    first = rounded(high)
    low = value - high
    third = rounded(low)
    return high, low, [first, high - first, third, low - third]


def star_rows(block):
    row = lax.broadcasted_iota(jnp.int32, block.shape, 0)

    def roll(value, shift):
        return pltpu.roll(value, shift, 0)

    moving = jnp.where(row < 6, block, 0.0)
    high, low, p = grid_pieces(moving)
    square = high * high
    twice = low * (2.0 * high + low)
    coarse = roll(square, 6) + roll(square, 5) + roll(square, 4)
    fine = roll(twice, 7) + roll(twice, 6) + roll(twice, 5)
    own = pieces(jnp.where(row == 6, coarse, jnp.where(row == 7, fine, 0.0)))
    both = moving * roll(moving, 5)
    cross = both + roll(both, 7) + roll(both, 6)
    c = pieces(jnp.broadcast_to(cross[0:1], cross.shape))
    last = jnp.where(row < 6, roll(block, 3), 0.0)
    for k in range(3):
        last = jnp.where(row == k, c[k], last)
    stack = []
    for k in range(3):
        stack += [p[k] + own[k]] * 4
    stack += [jnp.where(row == 6, 1.0, p[3])] * 3 + [last]
    return jnp.concatenate(stack, 0)


def sum3(rows):
    return rows[0:1] + rows[1:2] + rows[2:3]


def active_rows(pack):
    n = pack.shape[1]
    high, low, p = grid_pieces(pack)
    coarse = pieces(sum3(high[0:3] * high[0:3]))
    fine = pieces(sum3(low[0:3] * (2.0 * high[0:3] + low[0:3])) + SOFTEN2)
    cross = pieces(sum3(pack[0:3] * pack[3:6]))
    zero3, zero, one = jnp.zeros((3, n), F32), jnp.zeros((1, n), F32), jnp.ones((1, n), F32)
    ra, rb, rc = [], [], []
    for k in range(4):
        for l in range(4 if k < 3 else 3):
            is_coarse = k < 2 and l < 2
            unit = one if (l == 0 and k < 3) else zero
            twice = -2.0 * p[l][0:3]
            last = k == 3
            ra.append(jnp.concatenate([twice if is_coarse else zero3, zero3, coarse[l] if last else unit, zero], 0))
            rb.append(jnp.concatenate([zero3 if is_coarse else twice, zero3, fine[l] if last else zero, unit], 0))
            rc.append(jnp.concatenate([-p[l][3:6], -p[l][0:3], cross[l] if last else zero, zero], 0))
    ra.append(jnp.zeros((8, n), F32))
    rb.append(jnp.zeros((8, n), F32))
    rc.append(jnp.concatenate([jnp.ones((3, n), F32), jnp.zeros((5, n), F32)], 0))
    return [jnp.concatenate(rows, 0) for rows in (ra, rb, rc)]


def heavy_rows(block):
    row = lax.broadcasted_iota(jnp.int32, block.shape, 0)
    heavy = jnp.where(row == 6, block, block * block[6:7])
    return jnp.concatenate(pieces(heavy), 0).astype(BF16)


def force_kernel(
    stars_ref, state_ref, slot_ref, owner_ref, out_ref, met_ref, act_ref, mid_ref, sum_ref, feat_ref, prod_ref, weight_ref, col_ref
):
    n_tiles = stars_ref.shape[0]
    n_blocks = N_YLO * N_CORE
    n_team = state_ref.shape[0] // n_blocks
    n_act = n_blocks * LANES
    sides = range(0, n_act, SIDE)

    for b in range(n_blocks):
        state = state_ref[b]
        for t in range(1, n_team):
            state = state + state_ref[t * n_blocks + b]
        state = in_rows(state, N_STATE)
        xi, vi = predict(state[0:3], state[3:6], state[6:9], state[9:12], state[12:13])
        pack = jnp.concatenate([xi, vi, jnp.zeros((2, LANES), F32)], 0)
        act_ref[:, b * LANES : (b + 1) * LANES] = pack

    mean = jnp.sum(act_ref[...], axis=1, keepdims=True) * (1.0 / n_act)
    mid_ref[...] = jnp.broadcast_to(jnp.round(mean * 2.0) * 0.5, mid_ref.shape)
    for b in range(n_blocks):
        at = b * LANES
        pack = act_ref[:, at : at + LANES] - mid_ref[:, :LANES]
        act_ref[:, at : at + LANES] = pack
        for k, rows in enumerate(active_rows(pack)):
            met_ref[:, k * n_act + at : k * n_act + at + LANES] = rows.astype(BF16)

    def block_of(t):
        line = stars_ref[t]
        members = line.shape[1] // 7
        rows = [line[:, q * members : (q + 1) * members] for q in range(7)]
        return jnp.concatenate(rows + [jnp.zeros((1, members), F32)], 0) - mid_ref[...]

    def on_matrix(tile, side):
        return side < n_act // 2 or tile % CYCLE != CYCLE - 1

    def prepare(t, tile):
        cols = star_rows(block_of(t)).T
        feat_ref[...] = cols.astype(BF16)
        if not on_matrix(tile, n_act - 1):
            col_ref[...] = cols

    def products(side, tile):
        for k in (0, 1, 2) if on_matrix(tile, side) else (2,):
            at = k * n_act + side
            prod_ref[:, at : at + SIDE] = jnp.dot(
                feat_ref[...], met_ref[:, at : at + SIDE], preferred_element_type=F32
            )

    def weights(side, tile, same=None):
        cross = prod_ref[:, 2 * n_act + side : 2 * n_act + side + SIDE]
        if on_matrix(tile, side):
            r2 = prod_ref[:, side : side + SIDE] + prod_ref[:, n_act + side : n_act + side + SIDE]
        else:
            cols = col_ref[...]
            d = [cols[:, 123 + q : 124 + q] - act_ref[q : q + 1, side : side + SIDE] for q in range(3)]
            r2 = d[0] * d[0] + d[1] * d[1] + d[2] * d[2] + SOFTEN2
        inv = lax.rsqrt(r2)
        inv2 = inv * inv
        w = inv * inv2
        u = w * inv2 * cross
        if same is not None:
            w, u = (jnp.where(same[:, side : side + SIDE], 0.0, value) for value in (w, u))
        for k, value in enumerate((w, u)):
            upper = value.astype(BF16)
            at = 2 * k * n_act + side
            weight_ref[:, at : at + SIDE] = upper
            at = at + n_act
            weight_ref[:, at : at + SIDE] = (value - upper.astype(F32)).astype(BF16)

    def add_up(heavy, side):
        for k in range(2):
            at = 2 * k * n_act + side
            upper, lower = weight_ref[:, at : at + SIDE], weight_ref[:, at + n_act : at + n_act + SIDE]
            part = jnp.dot(heavy, upper, preferred_element_type=F32) + jnp.dot(
                heavy, lower, preferred_element_type=F32
            )
            at = k * n_act + side
            sum_ref[:, at : at + SIDE] = sum_ref[:, at : at + SIDE] + part

    here = lax.axis_index("x") * N_Z + lax.axis_index("z")
    mine = lax.axis_index("y") * N_CORE + lax.axis_index("core")
    wanted = jnp.where(owner_ref[...] == lax.axis_index("team"), slot_ref[...], -1)
    wanted = jnp.concatenate([jnp.where(mine == b, wanted, -1) for b in range(n_blocks)], 1)
    sum_ref[...] = jnp.zeros_like(sum_ref)

    def nth(t):
        return lax.rem(here + t, n_tiles)

    prepare(nth(0), 0)
    for side in sides:
        products(side, 0)
    prepare(nth(1), 1)

    def one_cycle(c, _):
        for tile in range(CYCLE):
            t = c * CYCLE + tile
            heavy = heavy_rows(block_of(nth(t)))
            same = None
            if tile == 0:
                star = lax.broadcasted_iota(jnp.int32, (feat_ref.shape[0], n_act), 0)
                same = star == jnp.where(c == 0, wanted, -1)
            for side in sides:
                weights(side, tile, same)
                products(side, tile + 1)
                add_up(heavy, side)
            prepare(nth(jnp.minimum(t + 2, n_tiles - 1)), tile + 2)
        return 0

    lax.fori_loop(0, n_tiles // CYCLE, one_cycle, 0, unroll=2)
    sums = sum_ref[16:24, :] + sum_ref[8:16, :] + sum_ref[0:8, :]
    sw, su = sums[:, :n_act], sums[:, n_act:]
    xi, vi = act_ref[0:3, :], act_ref[3:6, :]
    a = sw[0:3] - xi * sw[6:7]
    j = (sw[3:6] - vi * sw[6:7]) - 3.0 * (su[0:3] - xi * su[6:7])
    part = jnp.concatenate([a, j], 0)
    for b in range(n_blocks):
        line = in_line(part[:, b * LANES : (b + 1) * LANES], N_FORCE)
        for t in range(n_team):
            out_ref[t * n_blocks + b] = line


def correct_kernel(part_ref, state_ref, phase_ref, force_ref, higher_ref):
    n = part_ref.shape[0]
    n_blocks = N_YLO * N_CORE
    mine = lax.axis_index("y") * N_CORE + lax.axis_index("core")
    total = part_ref[0]
    for k in range(1, n):
        total = total + part_ref[k]
    own = state_ref[mine]
    for t in range(1, n // n_blocks):
        own = own + state_ref[t * n_blocks + mine]
    own, total = in_rows(own, N_STATE), in_rows(total, N_FORCE)
    x0, v0, a0, j0, dt = (own[0:3], own[3:6], own[6:9], own[9:12], own[12:13])
    a1, j1 = (total[0:3], total[3:6])
    v1 = v0 + (a0 + a1) * dt / 2.0 + (j0 - j1) * dt * dt / 12.0
    x1 = x0 + (v0 + v1) * dt / 2.0 + (a0 - a1) * dt * dt / 12.0
    snap = -6.0 * (a0 - a1) - dt * (4.0 * j0 + 2.0 * j1)
    crackle = 12.0 * (a0 - a1) + 6.0 * dt * (j0 + j1)
    phase_ref[...] = jnp.concatenate([x1, v1], 0)
    force_ref[...] = total[0:6]
    higher_ref[...] = jnp.concatenate([snap, crackle], 0)


def shards(sizes, position, velocity, old_accel, old_jerk, mass, elapsed, active_slot, active_owner):
    members = position.shape[1]
    actives = active_slot.shape[0]
    n_gather = sizes["x"] * sizes["z"]
    n_reduce = sizes["team"] * sizes["y"] * sizes["core"]
    n_blocks = sizes["y"] * sizes["core"]
    elapsed = elapsed.reshape(1, members)
    state = pl.pallas_call(
        state_kernel,
        out_shape=jax.ShapeDtypeStruct((n_reduce, 1, N_STATE * actives), F32),
        compiler_params=pltpu.CompilerParams(vmem_limit_bytes=SMALL),
        name="state",
    )(
        position, velocity, old_accel, old_jerk, elapsed,
        active_slot.reshape(1, actives), active_owner.reshape(1, actives),
    )
    stars = pl.pallas_call(
        star_kernel,
        out_shape=jax.ShapeDtypeStruct((n_gather, 1, 7 * members), F32),
        name="stars",
    )(position, velocity, old_accel, old_jerk, mass.reshape(1, members), elapsed)
    stars = lax.all_to_all(stars, GATHER, 0, 0, tiled=True)
    state, stars = lax.optimization_barrier((state, stars))
    state = lax.all_to_all(state, REDUCE, 0, 0, tiled=True)
    n_act = n_blocks * actives
    part = pl.pallas_call(
        force_kernel,
        out_shape=jax.ShapeDtypeStruct((n_reduce, 1, N_FORCE * actives), F32),
        scratch_shapes=[
            pltpu.VMEM((LANES, 3 * n_act), BF16),
            pltpu.VMEM((8, n_act), F32),
            pltpu.VMEM((8, members), F32),
            pltpu.VMEM((24, 2 * n_act), F32),
            pltpu.VMEM((members, LANES), BF16),
            pltpu.VMEM((members, 3 * n_act), F32),
            pltpu.VMEM((members, 4 * n_act), BF16),
            pltpu.VMEM((members, LANES), F32),
        ],
        compiler_params=pltpu.CompilerParams(vmem_limit_bytes=16 * 1024 * 1024),
        name="force",
    )(stars, state, active_slot.reshape(1, actives), active_owner.reshape(1, actives))
    part = lax.all_to_all(part, REDUCE, 0, 0, tiled=True)
    out = jax.ShapeDtypeStruct((6, actives), F32)
    return pl.pallas_call(
        correct_kernel,
        out_shape=(out, out, out),
        compiler_params=pltpu.CompilerParams(vmem_limit_bytes=SMALL),
        name="correct",
    )(part, state)


def solution(mesh):
    n_team = mesh.shape["team"]
    fine = Mesh(
        mesh.devices.reshape(n_team, N_X, N_YLO, N_Z, N_CORE), ("team", "x", "y", "z", "core")
    )
    blk = ("x", "y", "z", "core")
    whole = ("team",) + blk
    placed = (
        P(None, whole), P(None, whole), P(None, whole), P(None, whole),
        P(whole), P(whole), P(blk), P(blk),
    )
    return jax.shard_map(
        functools.partial(shards, dict(fine.shape)),
        mesh=fine,
        in_specs=placed,
        out_specs=(P(None, blk), P(None, blk), P(None, blk)),
        check_vma=False,
    )
```
